512 devices in a mesh: tracer: 32 (over y, z_hi, core), space: 16 (over z_lo, x).
Axes of the slice: x: 4, y: 8, z: 8 (z_hi: 2, z_lo: 4; z = z_hi * 4 + z_lo), core: 2. Of those that a mesh axis runs over, the one named last changes fastest.
Arguments:
- tracers: float32 [256, 4, 384, 256], P('tracer', None, 'space'), may hold values from -6 to 6
- thickness: float32 [4, 384, 256], P(None, 'space', 'tracer'), may hold values from 0.5 to 1.5
- wind_x: float32 [4, 384, 256], P(None, 'space', 'tracer'), may hold values from -3 to 3
- wind_y: float32 [4, 384, 256], P(None, 'space', 'tracer'), may hold values from -3 to 3
Outputs:
- tracers_out: float32 [256, 4, 384, 256], P('tracer', None, 'space')
- thickness_out: float32 [4, 384, 256], P(None, 'space', 'tracer')
The draws below stay inside these ranges and needn't reach their ends.
All inputs are finite; a program needn't handle non-finite values.
Results may differ from the reference program's by a relative error of at most 0.0003.
Values sent between devices are 32-bit elements; how exact they have to be, the bound alone decides.
No kernel may reach another device: no remote copies, remote signals or barrier semaphores. Data moves between devices by JAX's collectives and lax.ppermute only.
A program may use at most 64 MiB of HBM per device.

```python
import jax
import jax.numpy as jnp

LEV = 4
SUBSTEPS = 2
NTR = 256
NX = 384
NY = 256


def block_levels(key, dims, pieces, least, top_value):
    def one(position, parts):
        heights = jax.random.uniform(jax.random.fold_in(jax.random.fold_in(key, 6), position), (parts,), jnp.float32, least / len(pieces), top_value / len(pieces))
        return jnp.repeat(jnp.exp(heights), dims[position] // parts).reshape((-1,) + (1,) * (len(dims) - position - 1))

    level = one(*pieces[0])
    for cut in pieces[1:]:
        level = level * one(*cut)
    return level


def normal_values(stream_key, extent, scale, most, shards=(), kind=jnp.bfloat16):
    gain = block_levels(stream_key, extent, shards, -0.22, 0.18) if shards else 1.0
    values = jax.random.normal(stream_key, extent, jnp.float32) * scale * gain
    return jnp.minimum(jnp.maximum(values, -most), most).astype(kind)


def setup_inputs(seed: int = 0) -> dict:
    splits = jax.random.split(jax.random.key(seed), 5)
    tracers = normal_values(splits[0], (NTR, LEV, NX, NY), 1.0, 6.0, ((0, 32), (2, 16)), jnp.float32)
    thickness = jnp.clip(0.5 + 1.0 * jax.random.uniform(splits[1], (LEV, NX, NY), jnp.float32) ** block_levels(splits[1], (LEV, NX, NY), ((1, 16), (2, 32)), -0.2, 0.2), 0.5, 1.5)
    wind_x = jnp.clip(jax.random.uniform(splits[2], (LEV, NX, NY), jnp.float32, -3.0, 3.0) * block_levels(splits[2], (LEV, NX, NY), ((1, 16), (2, 32)), -0.4, 0.0), -3.0, 3.0)
    wind_y = jnp.clip(jax.random.uniform(splits[3], (LEV, NX, NY), jnp.float32, -3.0, 3.0) * block_levels(splits[3], (LEV, NX, NY), ((1, 16), (2, 32)), -0.4, 0.0), -3.0, 3.0)
    return dict(tracers=tracers, thickness=thickness, wind_x=wind_x, wind_y=wind_y)


courant_scale = 0.025


def slab(array, start, size, axis):
    index = [slice(None)] * array.ndim
    index[axis] = slice(start, start + size)
    return array[tuple(index)]


def face_values(padded, courant, count, axis):
    width = count + 3
    edges = (7.0 / 12.0) * (slab(padded, 1, width, axis) + slab(padded, 2, width, axis)) - (1.0 / 12.0) * (slab(padded, 0, width, axis) + slab(padded, 3, width, axis))
    left_low = slab(edges, 0, count + 1, axis)
    left_high = slab(edges, 1, count + 1, axis)
    left_mean = slab(padded, 2, count + 1, axis)
    right_low = slab(edges, 1, count + 1, axis)
    right_high = slab(edges, 2, count + 1, axis)
    right_mean = slab(padded, 3, count + 1, axis)
    left_curve = 6.0 * left_mean - 3.0 * (left_low + left_high)
    right_curve = 6.0 * right_mean - 3.0 * (right_low + right_high)
    upwind_pos = left_high - 0.5 * courant * ((left_high - left_low) - (1.0 - courant * (2.0 / 3.0)) * left_curve)
    upwind_neg = right_low - 0.5 * courant * ((right_high - right_low) + (1.0 + courant * (2.0 / 3.0)) * right_curve)
    return jnp.where(courant > 0, upwind_pos, upwind_neg)


def thin_out(thick, mass_flux, axis):
    count = thick.shape[axis]
    return thick - (slab(mass_flux, 1, count, axis) - slab(mass_flux, 0, count, axis))


def sweep(values, thick_old, thick_new, courant, mass_flux, padded, axis):
    count = values.shape[axis]
    flux = mass_flux * face_values(padded, courant, count, axis)
    change = slab(flux, 1, count, axis) - slab(flux, 0, count, axis)
    return (values * thick_old - change) / thick_new


def reference(tracers, thickness, wind_x, wind_y):
    rows = thickness.shape[1]
    cols = thickness.shape[2]
    levels = thickness.shape[0]
    row_index = jnp.arange(rows, dtype=jnp.int32)[:, None]
    col_index = jnp.arange(cols, dtype=jnp.int32)[None, :]
    cx = jnp.where(row_index > 0, courant_scale * wind_x, jnp.float32(0.0))
    cx = jnp.concatenate([cx, jnp.zeros((levels, 1, cols), jnp.float32)], axis=1)
    thick_pad = jnp.pad(thickness, ((0, 0), (1, 1), (0, 0)))
    mfx = cx * jnp.where(cx > 0, thick_pad[:, :-1], thick_pad[:, 1:])
    cy = jnp.where(col_index > 0, courant_scale * wind_y, jnp.float32(0.0))
    cy = jnp.concatenate([cy, jnp.zeros((levels, rows, 1), jnp.float32)], axis=2)
    thick_pad = jnp.pad(thickness, ((0, 0), (0, 0), (1, 1)))
    mfy = cy * jnp.where(cy > 0, thick_pad[:, :, :-1], thick_pad[:, :, 1:])
    values = tracers
    thick = thickness
    for step in range(SUBSTEPS):
        after_x = thin_out(thick, mfx, -2)
        padded = jnp.pad(values, ((0, 0), (0, 0), (3, 3), (0, 0)))
        values = sweep(values, thick, after_x, cx, mfx, padded, -2)
        after_y = thin_out(after_x, mfy, -1)
        padded = jnp.pad(values, ((0, 0), (0, 0), (0, 0), (3, 3)))
        values = sweep(values, after_x, after_y, cy, mfy, padded, -1)
        thick = after_y
    return values, thick
```

```python
import jax
import jax.numpy as jnp
from jax import lax
from jax.experimental import pallas as pl
from jax.experimental.pallas import tpu as pltpu
from jax.sharding import PartitionSpec as P

COURANT_SCALE = 0.025
LEV, ROWS, COLS, TR = 4, 24, 256, 8
BLOCK = 8
REACH = 3
HALO = 2 * REACH
SIDE = 4
SPAN = ROWS + 2 * SIDE
VMEM = pl.BlockSpec(memory_space=pltpu.VMEM)
PARAMS = pltpu.CompilerParams(vmem_limit_bytes=24 * 1024 * 1024)


def pack_fields(thick, wind_x, wind_y, packed):
    for f, field in enumerate((thick, wind_x, wind_y)):
        parts = []
        for l in range(LEV):
            own = field[l]
            parts += [own[:, ROWS - SIDE :], own, own[:, :SIDE]]
        packed[f] = jnp.concatenate(parts, axis=1)


def tile_rows(x):
    x = x.reshape(TR, LEV, ROWS // 8, 8, COLS // 128, 128)
    return jnp.transpose(x, (0, 1, 2, 4, 3, 5)).reshape(-1, 128)


def from_tile_rows(x):
    x = x.reshape(TR, LEV, ROWS // 8, COLS // 128, 8, 128)
    return jnp.transpose(x, (0, 1, 2, 4, 3, 5)).reshape(TR, LEV, ROWS, COLS)


def row_of_all(l, r, half):
    start = (l * (ROWS // 8) + r // 8) * (COLS // 128) * 8 + half * 8 + r % 8
    return pl.ds(start, TR, stride=LEV * ROWS * (COLS // 128))


def get_row(ref, l, r):
    return jnp.concatenate([ref[row_of_all(l, r, h), :] for h in range(2)], axis=1)


def pack_halos(tracers, low, high):
    for l in range(LEV):
        for r in range(HALO):
            low[l, r] = get_row(tracers, l, r)
            high[l, r] = get_row(tracers, l, ROWS - HALO + r)


def stencil(courant, flux, after):
    size = jnp.abs(courant)
    half = 0.5 * size
    curve = 3.0 * half * (1.0 - (2.0 / 3.0) * size)
    near = flux * (1.0 - half - curve)
    far = flux * (half - curve)
    mean = flux * (2.0 * curve)
    up = courant > 0
    far_l = jnp.where(up, far, 0.0)
    far_r = far - far_l
    mean_l = jnp.where(up, mean, 0.0)
    mean_r = mean - mean_l
    in_, out = 7.0 / 12.0, 1.0 / 12.0
    face = [
        -out * far_l,
        in_ * far_l - out * near,
        in_ * (far_l + near) - out * far_r + mean_l,
        in_ * (far_r + near) - out * far_l + mean_r,
        in_ * far_r - out * near,
        -out * far_r,
    ]
    moved = [after(w) for w in face]
    return (
        [face[0]]
        + [face[j] - moved[j - 1] for j in range(1, 6)]
        + [-moved[5]]
    )


def sweeps(
    gathered, tracers, low, high, out, thick_out, fields, mid, weights, ends, turned
):
    space = lax.axis_index("space")
    tracer = lax.axis_index("tracer")
    last_row = lax.axis_size("space") * ROWS
    for f in range(3):
        blocks = [
            gathered[c, j, f * BLOCK : (f + 1) * BLOCK, :]
            for j in range(16)
            for c in range(2)
        ]
        fields[f] = jnp.concatenate(blocks, axis=0).T

    row = lax.broadcasted_iota(jnp.int32, (SPAN, COLS), 0) + (space * ROWS - SIDE)
    col = lax.broadcasted_iota(jnp.int32, (SPAN, COLS), 1)

    def level(l, carry):
        at = pl.ds(pl.multiple_of(l * SPAN, SPAN), SPAN)
        inside = (row >= 0) & (row < last_row)
        thick = jnp.where(inside, fields[0, at, :], 1.0)
        next_row = lambda x: pltpu.roll(x, SPAN - 1, 0)
        next_col = lambda x: pltpu.roll(x, COLS - 1, 1)

        cx = jnp.where((row > 0) & (row < last_row), COURANT_SCALE * fields[1, at, :], 0.0)
        mfx = cx * jnp.where(cx > 0, pltpu.roll(thick, 1, 0), thick)
        cy = jnp.where(col > 0, COURANT_SCALE * fields[2, at, :], 0.0)
        mfy = cy * jnp.where(cy > 0, pltpu.roll(thick, 1, 1), thick)
        thin_x = next_row(mfx) - mfx
        thin_y = next_col(mfy) - mfy
        dp1 = thick - thin_x
        dp2 = dp1 - thin_y
        dp3 = dp2 - thin_x
        dp4 = dp3 - thin_y
        ends[at, :] = dp4
        r1, r2, r3, r4 = 1.0 / dp1, 1.0 / dp2, 1.0 / dp3, 1.0 / dp4

        def put(n, j, add, r_a, dp_a, r_b, dp_b):
            if j == 3:
                weights[n, j] = (add + dp_a) * r_a
                weights[n + 2, j] = (add + dp_b) * r_b
            else:
                weights[n, j] = add * r_a
                weights[n + 2, j] = add * r_b

        for j, add in enumerate(stencil(cx, mfx, next_row)):
            put(0, j, add, r1, thick, r3, dp2)
        for j, add in enumerate(stencil(cy, mfy, next_col)):
            step = j - REACH
            if step < 0:
                add = jnp.where(col >= -step, add, 0.0)
            elif step > 0:
                add = jnp.where(col < COLS - step, add, 0.0)
            put(1, j, add, r2, dp1, r4, dp3)

        def weight(n, j, r):
            return weights[n, j, r + SIDE : r + SIDE + 1, :]

        def both(cells, n, r):
            total = weight(n, 0, r) * cells[0]
            for j in range(1, 7):
                total += weight(n, j, r) * cells[j]
            result = weight(n + 1, REACH, r) * total
            for j in range(7):
                if j != REACH:
                    shift = (REACH - j) % COLS
                    result += weight(n + 1, j, r) * pltpu.roll(total, shift, 1)
            return result

        def first(r):
            if r < 0:
                return low[l, r + HALO]
            if r >= ROWS:
                return high[l, r - ROWS]
            return get_row(tracers, l, r)

        window = [first(r) for r in range(-HALO, 0)]
        for r in range(-REACH, ROWS + REACH):
            window.append(first(r + REACH))
            mid[r + REACH] = both(window, 0, r)
            window.pop(0)
        window = [mid[r] for r in range(HALO)]
        for r in range(ROWS):
            window.append(mid[r + HALO])
            done = both(window, 2, r)
            for h in range(2):
                out[row_of_all(l, r, h), :] = done[:, h * 128 : (h + 1) * 128]
            window.pop(0)
        return carry

    lax.fori_loop(0, LEV, level, 0)
    turned[...] = ends[...].T
    block = turned[pl.ds(pl.multiple_of(tracer * BLOCK, BLOCK), BLOCK), :]
    for l in range(LEV):
        start = l * SPAN + SIDE
        thick_out[l] = block[:, start : start + ROWS]


def shape(*dims):
    return jax.ShapeDtypeStruct(dims, jnp.float32)


def both_ways(up, down):
    count = lax.axis_size("space")
    route = [(i, i + 1) for i in range(count - 1)]
    back = [(b, a) for a, b in route]
    return lax.ppermute(up, "space", route), lax.ppermute(down, "space", back)


def per_device(tracers, thickness, wind_x, wind_y):
    count = lax.axis_size("tracer")
    turn = lambda x: jnp.transpose(x, (0, 2, 1))
    packed = pl.pallas_call(
        pack_fields,
        out_shape=shape(3, BLOCK, LEV * SPAN),
        in_specs=[VMEM] * 3,
        out_specs=VMEM,
        compiler_params=PARAMS,
    )(turn(thickness), turn(wind_x), turn(wind_y))
    below, above = both_ways(packed, packed)

    flat = tile_rows(tracers)
    low, high = pl.pallas_call(
        pack_halos,
        out_shape=[shape(LEV, HALO, TR, COLS)] * 2,
        in_specs=[VMEM],
        out_specs=[VMEM] * 2,
        compiler_params=PARAMS,
    )(flat)
    from_below, from_above = both_ways(high, low)

    place = lax.broadcasted_iota(jnp.int32, packed.shape, 2) % SPAN
    packed = jnp.where(
        place < SIDE, below, jnp.where(place >= SIDE + ROWS, above, packed)
    ).reshape(3 * BLOCK, LEV * SPAN)
    same_core = [list(range(c, count, 2)) for c in range(2)]
    same_chip = [[i, i + 1] for i in range(0, count, 2)]
    copies = jnp.broadcast_to(packed, (count // 2,) + packed.shape)
    gathered = lax.all_to_all(copies, "tracer", 0, 0, axis_index_groups=same_core)
    gathered = lax.all_gather(gathered, "tracer", axis_index_groups=same_chip)

    values, thick = pl.pallas_call(
        sweeps,
        out_shape=[shape(TR * LEV * ROWS * 2, 128), shape(LEV, BLOCK, ROWS)],
        in_specs=[VMEM] * 4,
        out_specs=[VMEM] * 2,
        scratch_shapes=[
            pltpu.VMEM((3, LEV * SPAN, COLS), jnp.float32),
            pltpu.VMEM((ROWS + HALO, TR, COLS), jnp.float32),
            pltpu.VMEM((4, 7, SPAN, COLS), jnp.float32),
            pltpu.VMEM((LEV * SPAN, COLS), jnp.float32),
            pltpu.VMEM((COLS, LEV * SPAN), jnp.float32),
        ],
        compiler_params=PARAMS,
    )(gathered, flat, from_below, from_above)
    return from_tile_rows(values), turn(thick)


def solution(mesh):
    in_specs = (
        P("tracer", None, "space", None),
        P(None, "space", "tracer"),
        P(None, "space", "tracer"),
        P(None, "space", "tracer"),
    )
    out_specs = (P("tracer", None, "space", None), P(None, "space", "tracer"))
    return jax.shard_map(
        per_device, mesh=mesh, in_specs=in_specs, out_specs=out_specs, check_vma=False
    )
```

```python
import jax
import jax.numpy as jnp
from jax import lax
from jax.experimental import pallas as pl
from jax.experimental.pallas import tpu as pltpu
from jax.sharding import PartitionSpec as P

COURANT_SCALE = 0.025
LEV, ROWS, COLS, TR = 4, 24, 256, 8
BLOCK = 8
REACH = 3
HALO = 2 * REACH
SIDE = 4
SPAN = ROWS + 2 * SIDE
VMEM = pl.BlockSpec(memory_space=pltpu.VMEM)
PARAMS = pltpu.CompilerParams(vmem_limit_bytes=24 * 1024 * 1024)


def pack_fields(thick, wind_x, wind_y, packed, held, arrived):
    copies = [
        pltpu.make_async_copy(field, held.at[f], arrived.at[f])
        for f, field in enumerate((thick, wind_x, wind_y))
    ]
    for copy in copies:
        copy.start()
    for f, copy in enumerate(copies):
        copy.wait()
        parts = []
        for l in range(LEV):
            own = held[f, l]
            parts += [own[:, ROWS - SIDE :], own, own[:, :SIDE]]
        packed[f] = jnp.concatenate(parts, axis=1)


def spread(pair, copies):
    core = lax.axis_index("tracer") % 2
    place = lax.broadcasted_iota(jnp.int32, (BLOCK, LEV * SPAN), 1) % SPAN
    half = copies.shape[0] // 2
    for f in range(3):
        here = slice(f * BLOCK, (f + 1) * BLOCK)
        first, second = pair[0, f], pair[1, f]
        own = jnp.where(core == 0, first, second)
        last_rows = jnp.where(place < SIDE, first, pltpu.roll(second, SIDE, 1))
        first_rows = jnp.where(
            place >= SPAN - SIDE, second, pltpu.roll(first, LEV * SPAN - SIDE, 1)
        )
        beside = jnp.where(core == 0, last_rows, first_rows)
        to_first = jnp.where(core == 0, own, beside)
        to_second = jnp.where(core == 0, beside, own)
        for i in range(half):
            copies[i, here, :] = to_first
            copies[half + i, here, :] = to_second


def tile_rows(x):
    x = x.reshape(TR, LEV, ROWS // 8, 8, COLS // 128, 128)
    return jnp.transpose(x, (0, 1, 2, 4, 3, 5)).reshape(-1, 128)


def from_tile_rows(x):
    x = x.reshape(TR, LEV, ROWS // 8, COLS // 128, 8, 128)
    return jnp.transpose(x, (0, 1, 2, 4, 3, 5)).reshape(TR, LEV, ROWS, COLS)


def row_of_all(l, r, half):
    start = (l * (ROWS // 8) + r // 8) * (COLS // 128) * 8 + half * 8 + r % 8
    return pl.ds(start, TR, stride=LEV * ROWS * (COLS // 128))


def get_row(ref, l, r):
    return jnp.concatenate([ref[row_of_all(l, r, h), :] for h in range(2)], axis=1)


def pack_halos(tracers, once, twice):
    odd = lax.axis_index("space") % 2 == 1
    for l in range(LEV):
        for r in range(HALO):
            low = get_row(tracers, l, r)
            high = get_row(tracers, l, ROWS - HALO + r)
            once[l, r] = jnp.where(odd, low, high)
            twice[l, r] = jnp.where(odd, high, low)


def stencil(courant, flux, after):
    size = jnp.abs(courant)
    half = 0.5 * size
    curve = 3.0 * half * (1.0 - (2.0 / 3.0) * size)
    near = flux * (1.0 - half - curve)
    far = flux * (half - curve)
    mean = flux * (2.0 * curve)
    up = courant > 0
    far_l = jnp.where(up, far, 0.0)
    far_r = far - far_l
    mean_l = jnp.where(up, mean, 0.0)
    mean_r = mean - mean_l
    in_, out = 7.0 / 12.0, 1.0 / 12.0
    face = [
        -out * far_l,
        in_ * far_l - out * near,
        in_ * (far_l + near) - out * far_r + mean_l,
        in_ * (far_r + near) - out * far_l + mean_r,
        in_ * far_r - out * near,
        -out * far_r,
    ]
    moved = [after(w) for w in face]
    return (
        [face[0]]
        + [face[j] - moved[j - 1] for j in range(1, 6)]
        + [-moved[5]]
    )


def sweeps(
    gathered, tracers, once, twice, out, thick_out, fields, mid, weights, ends, turned
):
    space = lax.axis_index("space")
    tracer = lax.axis_index("tracer")
    last_row = lax.axis_size("space") * ROWS
    odd = space % 2 == 1
    half = gathered.shape[1] // 2
    place = lax.broadcasted_iota(jnp.int32, (BLOCK, LEV * SPAN), 1) % SPAN
    for f in range(3):
        here = slice(f * BLOCK, (f + 1) * BLOCK)
        blocks = []
        for j in range(half):
            before = gathered[1, j, here, :]
            after = gathered[0, half + j, here, :]
            for own, below, above in (
                (gathered[0, j, here, :], before, pltpu.roll(after, SIDE, 1)),
                (
                    gathered[1, half + j, here, :],
                    pltpu.roll(before, LEV * SPAN - SIDE, 1),
                    after,
                ),
            ):
                own = jnp.where(place < SIDE, below, own)
                blocks.append(jnp.where(place >= SPAN - SIDE, above, own))
        fields[f] = jnp.concatenate(blocks, axis=0).T

    row = lax.broadcasted_iota(jnp.int32, (SPAN, COLS), 0) + (space * ROWS - SIDE)
    col = lax.broadcasted_iota(jnp.int32, (SPAN, COLS), 1)

    def level(l, carry):
        at = pl.ds(pl.multiple_of(l * SPAN, SPAN), SPAN)
        inside = (row >= 0) & (row < last_row)
        thick = jnp.where(inside, fields[0, at, :], 1.0)
        next_row = lambda x: pltpu.roll(x, SPAN - 1, 0)
        next_col = lambda x: pltpu.roll(x, COLS - 1, 1)

        cx = jnp.where((row > 0) & (row < last_row), COURANT_SCALE * fields[1, at, :], 0.0)
        mfx = cx * jnp.where(cx > 0, pltpu.roll(thick, 1, 0), thick)
        cy = jnp.where(inside & (col > 0), COURANT_SCALE * fields[2, at, :], 0.0)
        mfy = cy * jnp.where(cy > 0, pltpu.roll(thick, 1, 1), thick)
        thin_x = next_row(mfx) - mfx
        thin_y = next_col(mfy) - mfy
        dp1 = thick - thin_x
        dp2 = dp1 - thin_y
        dp3 = dp2 - thin_x
        dp4 = dp3 - thin_y
        ends[at, :] = dp4
        r1, r2, r3, r4 = 1.0 / dp1, 1.0 / dp2, 1.0 / dp3, 1.0 / dp4

        def put(n, j, add, r_a, dp_a, r_b, dp_b):
            if j == 3:
                weights[n, j] = (add + dp_a) * r_a
                weights[n + 2, j] = (add + dp_b) * r_b
            else:
                weights[n, j] = add * r_a
                weights[n + 2, j] = add * r_b

        for j, add in enumerate(stencil(cx, mfx, next_row)):
            put(0, j, add, r1, thick, r3, dp2)
        for j, add in enumerate(stencil(cy, mfy, next_col)):
            step = j - REACH
            if step < 0:
                add = jnp.where(col >= -step, add, 0.0)
            elif step > 0:
                add = jnp.where(col < COLS - step, add, 0.0)
            put(1, j, add, r2, dp1, r4, dp3)

        def weight(n, j, r):
            return weights[n, j, r + SIDE : r + SIDE + 1, :]

        def both(cells, n, r):
            total = weight(n, 0, r) * cells[0]
            for j in range(1, 7):
                total += weight(n, j, r) * cells[j]
            result = weight(n + 1, REACH, r) * total
            for j in range(7):
                if j != REACH:
                    shift = (REACH - j) % COLS
                    result += weight(n + 1, j, r) * pltpu.roll(total, shift, 1)
            return result

        def first(r):
            if r < 0:
                return jnp.where(odd, once[l, r + HALO], twice[l, r + HALO])
            if r >= ROWS:
                return jnp.where(odd, twice[l, r - ROWS], once[l, r - ROWS])
            return get_row(tracers, l, r)

        window = [first(r) for r in range(-HALO, 0)]
        for r in range(-REACH, ROWS + REACH):
            window.append(first(r + REACH))
            mid[r + REACH] = both(window, 0, r)
            window.pop(0)
        window = [mid[r] for r in range(HALO)]
        for r in range(ROWS):
            window.append(mid[r + HALO])
            done = both(window, 2, r)
            for h in range(2):
                out[row_of_all(l, r, h), :] = done[:, h * 128 : (h + 1) * 128]
            window.pop(0)
        return carry

    lax.fori_loop(0, LEV, level, 0)
    turned[...] = ends[...].T
    block = turned[pl.ds(pl.multiple_of(tracer * BLOCK, BLOCK), BLOCK), :]
    for l in range(LEV):
        start = l * SPAN + SIDE
        thick_out[l] = block[:, start : start + ROWS]


def shape(*dims):
    return jax.ShapeDtypeStruct(dims, jnp.float32)


def swap(block, start):
    count = lax.axis_size("space")
    pairs = [(i, i + 1) for i in range(start, count - 1, 2)]
    return lax.ppermute(block, "space", pairs + [(b, a) for a, b in pairs])


def per_device(tracers, thickness, wind_x, wind_y):
    count, steps = lax.axis_size("tracer"), lax.axis_size("space")
    turn = lambda x: jnp.transpose(x, (0, 2, 1))
    packed = pl.pallas_call(
        pack_fields,
        out_shape=shape(3, BLOCK, LEV * SPAN),
        in_specs=[pl.BlockSpec(memory_space=pl.ANY)] * 3,
        out_specs=VMEM,
        scratch_shapes=[
            pltpu.VMEM((3, LEV, BLOCK, ROWS), jnp.float32),
            pltpu.SemaphoreType.DMA((3,)),
        ],
    )(turn(thickness), turn(wind_x), turn(wind_y))
    same_chip = [[i, i + 1] for i in range(0, count, 2)]
    pair = lax.all_gather(packed, "tracer", axis_index_groups=same_chip)
    copies = pl.pallas_call(
        spread,
        out_shape=shape(count, 3 * BLOCK, LEV * SPAN),
        in_specs=[VMEM],
        out_specs=VMEM,
        compiler_params=PARAMS,
    )(pair)
    members = [
        [
            (2 * j + core) * steps + (place + core) % steps
            for core in range(2)
            for j in range(count // 2)
        ]
        for place in range(steps)
    ]
    gathered = lax.all_to_all(
        copies, ("tracer", "space"), 0, 0, axis_index_groups=members
    )
    gathered = lax.all_gather(gathered, "tracer", axis_index_groups=same_chip)

    flat = tile_rows(tracers)
    once, twice = pl.pallas_call(
        pack_halos,
        out_shape=[shape(LEV, HALO, TR, COLS)] * 2,
        in_specs=[VMEM],
        out_specs=[VMEM] * 2,
        compiler_params=PARAMS,
    )(flat)
    once, twice = swap(once, 0), swap(twice, 1)

    values, thick = pl.pallas_call(
        sweeps,
        out_shape=[shape(TR * LEV * ROWS * 2, 128), shape(LEV, BLOCK, ROWS)],
        in_specs=[VMEM] * 4,
        out_specs=[VMEM] * 2,
        scratch_shapes=[
            pltpu.VMEM((3, LEV * SPAN, COLS), jnp.float32),
            pltpu.VMEM((ROWS + HALO, TR, COLS), jnp.float32),
            pltpu.VMEM((4, 7, SPAN, COLS), jnp.float32),
            pltpu.VMEM((LEV * SPAN, COLS), jnp.float32),
            pltpu.VMEM((COLS, LEV * SPAN), jnp.float32),
        ],
        compiler_params=PARAMS,
    )(gathered, flat, once, twice)
    return from_tile_rows(values), turn(thick)


def solution(mesh):
    in_specs = (
        P("tracer", None, "space", None),
        P(None, "space", "tracer"),
        P(None, "space", "tracer"),
        P(None, "space", "tracer"),
    )
    out_specs = (P("tracer", None, "space", None), P(None, "space", "tracer"))
    return jax.shard_map(
        per_device, mesh=mesh, in_specs=in_specs, out_specs=out_specs, check_vma=False
    )
```

```python
import jax
import jax.numpy as jnp
from jax import lax
from jax.experimental import pallas as pl
from jax.experimental.pallas import tpu as pltpu
from jax.sharding import PartitionSpec as P

COURANT_SCALE = 0.025
SUBSTEPS = 2
LEV, ROWS, COLS, TR = 4, 24, 256, 8
HALVES = COLS // 128
TOGETHER = 2
BLOCK = 8
REACH = 3
HALO = 2 * REACH
SIDE = 4
SPAN = ROWS + 2 * SIDE
VMEM = pl.BlockSpec(memory_space=pltpu.VMEM)
PARAMS = pltpu.CompilerParams(vmem_limit_bytes=24 * 1024 * 1024)


def pack_fields(thick, wind_x, wind_y, packed, held, arrived):
    copies = [
        pltpu.make_async_copy(field, held.at[f], arrived.at[f])
        for f, field in enumerate((thick, wind_x, wind_y))
    ]
    for copy in copies:
        copy.start()
    for f, copy in enumerate(copies):
        copy.wait()
        parts = []
        for l in range(LEV):
            own = held[f, l]
            parts += [own[:, ROWS - SIDE :], own, own[:, :SIDE]]
        packed[f] = jnp.concatenate(parts, axis=1)


def spread(pair, copies):
    core = lax.axis_index("tracer") % 2
    place = lax.broadcasted_iota(jnp.int32, (BLOCK, LEV * SPAN), 1) % SPAN
    half = copies.shape[0] // 2
    for f in range(3):
        here = slice(f * BLOCK, (f + 1) * BLOCK)
        first, second = pair[0, f], pair[1, f]
        own = jnp.where(core == 0, first, second)
        last_rows = jnp.where(place < SIDE, first, pltpu.roll(second, SIDE, 1))
        first_rows = jnp.where(
            place >= SPAN - SIDE, second, pltpu.roll(first, LEV * SPAN - SIDE, 1)
        )
        beside = jnp.where(core == 0, last_rows, first_rows)
        to_first = jnp.where(core == 0, own, beside)
        to_second = jnp.where(core == 0, beside, own)
        for i in range(half):
            copies[i, here, :] = to_first
            copies[half + i, here, :] = to_second


def tile_rows(x):
    x = x.reshape(TR, LEV, ROWS // 8, 8, HALVES, 128)
    return jnp.transpose(x, (0, 1, 2, 4, 3, 5)).reshape(-1, 128)


def from_tile_rows(x):
    x = x.reshape(TR, LEV, ROWS // 8, HALVES, 8, 128)
    return jnp.transpose(x, (0, 1, 2, 4, 3, 5)).reshape(TR, LEV, ROWS, COLS)


def tile_of(t, l, tile, half):
    start = (((t * LEV + l) * (ROWS // 8) + tile) * HALVES + half) * 8
    return pl.ds(pl.multiple_of(start, 8), 8)


def halo_of(t, half):
    return pl.ds((t * HALVES + half) * HALO, HALO)


def pack_halos(tracers, once, twice):
    odd = lax.axis_index("space") % 2 == 1
    for l in range(LEV):
        for t in range(TR):
            for h in range(HALVES):
                low = tracers[tile_of(t, l, 0, h), :][:HALO]
                high = tracers[tile_of(t, l, ROWS // 8 - 1, h), :][8 - HALO :]
                once[l, halo_of(t, h), :] = jnp.where(odd, low, high)
                twice[l, halo_of(t, h), :] = jnp.where(odd, high, low)


def stencil(courant, flux, after):
    size = jnp.abs(courant)
    half = 0.5 * size
    curve = 3.0 * half * (1.0 - (2.0 / 3.0) * size)
    near = flux * (1.0 - half - curve)
    far = flux * (half - curve)
    mean = flux * (2.0 * curve)
    up = courant > 0
    far_l = jnp.where(up, far, 0.0)
    far_r = far - far_l
    mean_l = jnp.where(up, mean, 0.0)
    mean_r = mean - mean_l
    in_, out = 7.0 / 12.0, 1.0 / 12.0
    face = [
        -out * far_l,
        in_ * far_l - out * near,
        in_ * (far_l + near) - out * far_r + mean_l,
        in_ * (far_r + near) - out * far_l + mean_r,
        in_ * far_r - out * near,
        -out * far_r,
    ]
    moved = [after(w) for w in face]
    return (
        [face[0]]
        + [face[j] - moved[j - 1] for j in range(1, 6)]
        + [-moved[5]]
    )


def sweeps(
    gathered,
    tracers,
    once,
    twice,
    out,
    thick_out,
    fields,
    cells,
    mid,
    weights,
    thin,
    ends,
    turned,
    staged,
    left,
):
    space = lax.axis_index("space")
    tracer = lax.axis_index("tracer")
    last_row = lax.axis_size("space") * ROWS
    odd = space % 2 == 1
    half = gathered.shape[1] // 2
    place = lax.broadcasted_iota(jnp.int32, (BLOCK, LEV * SPAN), 1) % SPAN
    for f in range(3):
        here = slice(f * BLOCK, (f + 1) * BLOCK)
        blocks = []
        for j in range(half):
            before = gathered[1, j, here, :]
            after = gathered[0, half + j, here, :]
            for own, below, above in (
                (gathered[0, j, here, :], before, pltpu.roll(after, SIDE, 1)),
                (
                    gathered[1, half + j, here, :],
                    pltpu.roll(before, LEV * SPAN - SIDE, 1),
                    after,
                ),
            ):
                own = jnp.where(place < SIDE, below, own)
                blocks.append(jnp.where(place >= SPAN - SIDE, above, own))
        fields[f] = jnp.concatenate(blocks, axis=0).T

    def copies_out(l):
        size = ROWS * HALVES
        for t in range(TR):
            at = pl.ds(pl.multiple_of((t * LEV + l) * size, size), size)
            yield pltpu.make_async_copy(staged.at[at], out.at[at], left.at[l, t])

    groups = [range(t, t + TOGETHER) for t in range(0, TR, TOGETHER)]
    tile_shape, half_shape = (8, COLS), (SPAN, 128)
    tile_row = lax.broadcasted_iota(jnp.int32, tile_shape, 0) + (space * ROWS - SIDE)
    col = lax.broadcasted_iota(jnp.int32, tile_shape, 1)
    row = lax.broadcasted_iota(jnp.int32, half_shape, 0) + (space * ROWS - SIDE)
    near = (-3, -2, -1, 1, 2, 3)

    def level(l, carry):
        base = pl.multiple_of(l * SPAN, SPAN)

        for tile in range(SPAN // 8):
            at = slice(8 * tile, 8 * tile + 8)
            field = lambda f: fields[f, pl.ds(base + 8 * tile, 8), :]
            next_col = lambda x: pltpu.roll(x, COLS - 1, 1)
            r = tile_row + 8 * tile
            inside = (r >= 0) & (r < last_row)
            thick = jnp.where(inside, field(0), 1.0)
            c = jnp.where(inside & (col > 0), COURANT_SCALE * field(2), 0.0)
            flux = c * jnp.where(c > 0, pltpu.roll(thick, 1, 1), thick)
            adds = stencil(c, flux, next_col)
            values = {"thin": next_col(flux) - flux, "own": adds[REACH]}
            for j, step in enumerate(near):
                add = adds[step + REACH]
                if step < 0:
                    add = jnp.where(col >= -step, add, 0.0)
                else:
                    add = jnp.where(col < COLS - step, add, 0.0)
                if abs(step) > 1:
                    add = pltpu.roll(add, REACH if step > 0 else COLS - REACH, 1)
                values[j] = add
            for h in range(HALVES):
                cut = slice(h * 128, (h + 1) * 128)
                thin[h, at, :] = values["thin"][:, cut]
                weights[1, 6, h, at, :] = values["own"][:, cut]
                for j in range(6):
                    weights[1, j, h, at, :] = values[j][:, cut]

        for h in range(HALVES):
            cut = slice(h * 128, (h + 1) * 128)
            field = lambda f: fields[f, pl.ds(base, SPAN), cut]
            next_row = lambda x: pltpu.roll(x, SPAN - 1, 0)
            inside = (row >= 0) & (row < last_row)
            thick = jnp.where(inside, field(0), 1.0)
            c = jnp.where((row > 0) & (row < last_row), COURANT_SCALE * field(1), 0.0)
            flux = c * jnp.where(c > 0, pltpu.roll(thick, 1, 0), thick)
            thin_x = next_row(flux) - flux
            adds = stencil(c, flux, next_row)
            for j, step in enumerate(near):
                weights[0, j, h] = adds[step + REACH]
            thin_y = thin[h]
            own = weights[1, 6, h]
            for substep in range(SUBSTEPS):
                weights[0, 6 + substep, h] = adds[REACH] + thick
                thick = thick - thin_x
                weights[0, 8 + substep, h] = 1.0 / thick
                weights[1, 6 + substep, h] = own + thick
                thick = thick - thin_y
                weights[1, 8 + substep, h] = 1.0 / thick
            ends[pl.ds(base, SPAN), cut] = thick

        for t in range(TR):
            for h in range(HALVES):
                for tile in range(ROWS // 8):
                    cells[t, h, 8 + 8 * tile : 16 + 8 * tile, :] = tracers[
                        tile_of(t, l, tile, h), :
                    ]
                one, two = once[l, halo_of(t, h), :], twice[l, halo_of(t, h), :]
                cells[t, h, 8 - HALO : 8, :] = jnp.where(odd, one, two)
                cells[t, h, 8 + ROWS : 8 + ROWS + HALO, :] = jnp.where(odd, two, one)

        def along(source, first, w):
            total = None
            for step in range(-REACH, REACH + 1):
                term = w[step] * source[first + step : first + step + 8, :]
                total = term if total is None else total + term
            return w["over"] * total

        def across(qs, w):
            left = [pltpu.roll(q, 1, 1) for q in qs]
            right = [pltpu.roll(q, COLS - 1, 1) for q in qs]
            up = [w[-3] * q + w[-2] * r for q, r in zip(qs, right)]
            down = [w[3] * q + w[2] * l for q, l in zip(qs, left)]
            up = [pltpu.roll(x, REACH, 1) for x in up]
            down = [pltpu.roll(x, COLS - REACH, 1) for x in down]
            return [
                w["over"] * (w[-1] * l + w[0] * q + w[1] * r + u + d)
                for l, q, r, u, d in zip(left, qs, right, up, down)
            ]

        names = dict(zip(near, range(6)))

        def row_weights(substep, first, h):
            all_names = names | {0: 6 + substep, "over": 8 + substep}
            at = slice(first, first + 8)
            return {n: weights[0, j, h, at, :] for n, j in all_names.items()}

        def col_weights(substep, first):
            all_names = names | {0: 6 + substep, "over": 8 + substep}
            at = slice(first, first + 8)
            return {
                n: jnp.concatenate([weights[1, j, h, at, :] for h in range(HALVES)], 1)
                for n, j in all_names.items()
            }

        def mid_at(t, h, tile):
            return mid.at[t, h, 8 * tile : 8 * tile + 8]

        def staged_at(t, h, tile):
            return staged.at[tile_of(t, l, tile, h)]

        def row_steps(substep, tile):
            first = 8 * tile + SIDE * substep
            for h in range(HALVES):
                w = row_weights(substep, first, h)
                for t in range(TR):
                    if substep == 0:
                        source, to, start = cells.at[t, h], mid_at, first + 8 - SIDE
                    else:
                        source, to, start = mid.at[t, h], staged_at, first
                    to(t, h, tile)[...] = along(source, start, w)
                    yield

        def col_steps(substep, tile):
            w = col_weights(substep, 8 * tile + SIDE * substep)
            at = (mid_at, staged_at)[substep]
            for ts in groups:
                qs = [
                    jnp.concatenate([at(t, h, tile)[...] for h in range(HALVES)], 1)
                    for t in ts
                ]
                for t, q in zip(ts, across(qs, w)):
                    for h in range(HALVES):
                        at(t, h, tile)[...] = q[:, h * 128 : (h + 1) * 128]
                yield

        def side_by_side(cols, rows):
            per = TR * HALVES // len(groups)
            while cols or rows:
                if cols and next(cols, 0) == 0:
                    cols = None
                for _ in range(per):
                    if rows and next(rows, 0) == 0:
                        rows = None

        for substep, tiles in ((0, SPAN // 8), (1, ROWS // 8)):
            cols = None
            for tile in range(tiles):
                side_by_side(cols, row_steps(substep, tile))
                cols = col_steps(substep, tile)
            side_by_side(cols, None)
        for copy in copies_out(l):
            copy.start()
        return carry

    lax.fori_loop(0, LEV, level, 0)
    turned[...] = ends[...].T
    block = turned[pl.ds(pl.multiple_of(tracer * BLOCK, BLOCK), BLOCK), :]
    for l in range(LEV):
        start = l * SPAN + SIDE
        thick_out[l] = block[:, start : start + ROWS]
    for l in range(LEV):
        for copy in copies_out(l):
            copy.wait()


def shape(*dims):
    return jax.ShapeDtypeStruct(dims, jnp.float32)


def swap(block, start):
    count = lax.axis_size("space")
    pairs = [(i, i + 1) for i in range(start, count - 1, 2)]
    return lax.ppermute(block, "space", pairs + [(b, a) for a, b in pairs])


def per_device(tracers, thickness, wind_x, wind_y):
    count, steps = lax.axis_size("tracer"), lax.axis_size("space")
    turn = lambda x: jnp.transpose(x, (0, 2, 1))
    packed = pl.pallas_call(
        pack_fields,
        out_shape=shape(3, BLOCK, LEV * SPAN),
        in_specs=[pl.BlockSpec(memory_space=pl.ANY)] * 3,
        out_specs=VMEM,
        scratch_shapes=[
            pltpu.VMEM((3, LEV, BLOCK, ROWS), jnp.float32),
            pltpu.SemaphoreType.DMA((3,)),
        ],
    )(turn(thickness), turn(wind_x), turn(wind_y))
    same_chip = [[i, i + 1] for i in range(0, count, 2)]
    pair = lax.all_gather(packed, "tracer", axis_index_groups=same_chip)
    copies = pl.pallas_call(
        spread,
        out_shape=shape(count, 3 * BLOCK, LEV * SPAN),
        in_specs=[VMEM],
        out_specs=VMEM,
        compiler_params=PARAMS,
    )(pair)
    members = [
        [
            (2 * j + core) * steps + (place + core) % steps
            for core in range(2)
            for j in range(count // 2)
        ]
        for place in range(steps)
    ]
    gathered = lax.all_to_all(
        copies, ("tracer", "space"), 0, 0, axis_index_groups=members
    )
    gathered = lax.all_gather(gathered, "tracer", axis_index_groups=same_chip)

    flat = tile_rows(tracers)
    once, twice = pl.pallas_call(
        pack_halos,
        out_shape=[shape(LEV, TR * HALVES * HALO, 128)] * 2,
        in_specs=[VMEM],
        out_specs=[VMEM] * 2,
        compiler_params=PARAMS,
    )(flat)
    once, twice = swap(once, 0), swap(twice, 1)

    values, thick = pl.pallas_call(
        sweeps,
        out_shape=[shape(TR * LEV * ROWS * HALVES, 128), shape(LEV, BLOCK, ROWS)],
        in_specs=[VMEM] * 4,
        out_specs=[pl.BlockSpec(memory_space=pl.ANY), VMEM],
        scratch_shapes=[
            pltpu.VMEM((3, LEV * SPAN, COLS), jnp.float32),
            pltpu.VMEM((TR, HALVES, ROWS + 16, 128), jnp.float32),
            pltpu.VMEM((TR, HALVES, SPAN, 128), jnp.float32),
            pltpu.VMEM((2, 10, HALVES, SPAN, 128), jnp.float32),
            pltpu.VMEM((HALVES, SPAN, 128), jnp.float32),
            pltpu.VMEM((LEV * SPAN, COLS), jnp.float32),
            pltpu.VMEM((COLS, LEV * SPAN), jnp.float32),
            pltpu.VMEM((TR * LEV * ROWS * HALVES, 128), jnp.float32),
            pltpu.SemaphoreType.DMA((LEV, TR)),
        ],
        compiler_params=PARAMS,
    )(gathered, flat, once, twice)
    return from_tile_rows(values), turn(thick)


def solution(mesh):
    in_specs = (
        P("tracer", None, "space", None),
        P(None, "space", "tracer"),
        P(None, "space", "tracer"),
        P(None, "space", "tracer"),
    )
    out_specs = (P("tracer", None, "space", None), P(None, "space", "tracer"))
    return jax.shard_map(
        per_device, mesh=mesh, in_specs=in_specs, out_specs=out_specs, check_vma=False
    )
```

```python
import jax
import jax.numpy as jnp
from jax import lax
from jax.experimental import pallas as pl
from jax.experimental.pallas import tpu as pltpu
from jax.sharding import PartitionSpec as P

COURANT_SCALE = 0.025
LEV, ROWS, COLS, TR = 4, 24, 256, 8
FIRST = 9
BLOCK = 8
REACH = 3
HALO = 2 * REACH
SIDE = 4
SPAN = ROWS + 2 * SIDE
VMEM = pl.BlockSpec(memory_space=pltpu.VMEM)
PARAMS = pltpu.CompilerParams(vmem_limit_bytes=24 * 1024 * 1024)


def pack_fields(thick, wind_x, wind_y, packed, held, arrived):
    copies = [
        pltpu.make_async_copy(field, held.at[f], arrived.at[f])
        for f, field in enumerate((thick, wind_x, wind_y))
    ]
    for copy in copies:
        copy.start()
    for f, copy in enumerate(copies):
        copy.wait()
        parts = []
        for l in range(LEV):
            own = held[f, l]
            parts += [own[:, ROWS - SIDE :], own, own[:, :SIDE]]
        packed[f] = jnp.concatenate(parts, axis=1)


def spread(pair, copies):
    core = lax.axis_index("tracer") % 2
    place = lax.broadcasted_iota(jnp.int32, (BLOCK, LEV * SPAN), 1) % SPAN
    half = copies.shape[0] // 2
    for f in range(3):
        here = slice(f * BLOCK, (f + 1) * BLOCK)
        first, second = pair[0, f], pair[1, f]
        own = jnp.where(core == 0, first, second)
        last_rows = jnp.where(place < SIDE, first, pltpu.roll(second, SIDE, 1))
        first_rows = jnp.where(
            place >= SPAN - SIDE, second, pltpu.roll(first, LEV * SPAN - SIDE, 1)
        )
        beside = jnp.where(core == 0, last_rows, first_rows)
        to_first = jnp.where(core == 0, own, beside)
        to_second = jnp.where(core == 0, beside, own)
        for i in range(half):
            copies[i, here, :] = to_first
            copies[half + i, here, :] = to_second


def tile_rows(x):
    x = x.reshape(TR, LEV, ROWS // 8, 8, COLS // 128, 128)
    return jnp.transpose(x, (0, 1, 2, 4, 3, 5)).reshape(-1, 128)


def from_tile_rows(x):
    x = x.reshape(TR, LEV, ROWS // 8, COLS // 128, 8, 128)
    return jnp.transpose(x, (0, 1, 2, 4, 3, 5)).reshape(TR, LEV, ROWS, COLS)


def row_of_all(l, r, half):
    start = (l * (ROWS // 8) + r // 8) * (COLS // 128) * 8 + half * 8 + r % 8
    return pl.ds(start, TR, stride=LEV * ROWS * (COLS // 128))


def get_row(ref, l, r):
    return jnp.concatenate([ref[row_of_all(l, r, h), :] for h in range(2)], axis=1)


def pack_halos(tracers, once, twice):
    odd = lax.axis_index("space") % 2 == 1
    for l in range(LEV):
        for r in range(HALO):
            low = get_row(tracers, l, r)
            high = get_row(tracers, l, ROWS - HALO + r)
            once[l, r] = jnp.where(odd, low, high)
            twice[l, r] = jnp.where(odd, high, low)


def stencil(courant, flux, after):
    size = jnp.abs(courant)
    half = 0.5 * size
    curve = 3.0 * half * (1.0 - (2.0 / 3.0) * size)
    near = flux * (1.0 - half - curve)
    far = flux * (half - curve)
    mean = flux * (2.0 * curve)
    up = courant > 0
    far_l = jnp.where(up, far, 0.0)
    far_r = far - far_l
    mean_l = jnp.where(up, mean, 0.0)
    mean_r = mean - mean_l
    in_, out = 7.0 / 12.0, 1.0 / 12.0
    face = [
        -out * far_l,
        in_ * far_l - out * near,
        in_ * (far_l + near) - out * far_r + mean_l,
        in_ * (far_r + near) - out * far_l + mean_r,
        in_ * far_r - out * near,
        -out * far_r,
    ]
    moved = [after(w) for w in face]
    return (
        [face[0]]
        + [face[j] - moved[j - 1] for j in range(1, 6)]
        + [-moved[5]]
    )


def sweeps(
    gathered, tracers, once, twice, out, thick_out, fields, mid, weights, ends, turned
):
    space = lax.axis_index("space")
    tracer = lax.axis_index("tracer")
    last_row = lax.axis_size("space") * ROWS
    odd = space % 2 == 1
    half = gathered.shape[1] // 2
    place = lax.broadcasted_iota(jnp.int32, (BLOCK, LEV * SPAN), 1) % SPAN
    for f in range(3):
        here = slice(f * BLOCK, (f + 1) * BLOCK)
        blocks = []
        for chip in range(half):
            j = (chip - FIRST) % half
            before = gathered[1, j, here, :]
            after = gathered[0, half + j, here, :]
            for own, below, above in (
                (gathered[0, j, here, :], before, pltpu.roll(after, SIDE, 1)),
                (
                    gathered[1, half + j, here, :],
                    pltpu.roll(before, LEV * SPAN - SIDE, 1),
                    after,
                ),
            ):
                own = jnp.where(place < SIDE, below, own)
                blocks.append(jnp.where(place >= SPAN - SIDE, above, own))
        fields[f] = jnp.concatenate(blocks, axis=0).T

    row = lax.broadcasted_iota(jnp.int32, (SPAN, COLS), 0) + (space * ROWS - SIDE)
    col = lax.broadcasted_iota(jnp.int32, (SPAN, COLS), 1)

    def level(l, carry):
        at = pl.ds(pl.multiple_of(l * SPAN, SPAN), SPAN)
        inside = (row >= 0) & (row < last_row)
        thick = jnp.where(inside, fields[0, at, :], 1.0)
        next_row = lambda x: pltpu.roll(x, SPAN - 1, 0)
        next_col = lambda x: pltpu.roll(x, COLS - 1, 1)

        cx = jnp.where((row > 0) & (row < last_row), COURANT_SCALE * fields[1, at, :], 0.0)
        mfx = cx * jnp.where(cx > 0, pltpu.roll(thick, 1, 0), thick)
        cy = jnp.where(inside & (col > 0), COURANT_SCALE * fields[2, at, :], 0.0)
        mfy = cy * jnp.where(cy > 0, pltpu.roll(thick, 1, 1), thick)
        thin_x = next_row(mfx) - mfx
        thin_y = next_col(mfy) - mfy
        dp1 = thick - thin_x
        dp2 = dp1 - thin_y
        dp3 = dp2 - thin_x
        dp4 = dp3 - thin_y
        ends[at, :] = dp4
        r1, r2, r3, r4 = 1.0 / dp1, 1.0 / dp2, 1.0 / dp3, 1.0 / dp4

        def put(n, j, add, r_a, dp_a, r_b, dp_b):
            if j == 3:
                weights[n, j] = (add + dp_a) * r_a
                weights[n + 2, j] = (add + dp_b) * r_b
            else:
                weights[n, j] = add * r_a
                weights[n + 2, j] = add * r_b

        for j, add in enumerate(stencil(cx, mfx, next_row)):
            put(0, j, add, r1, thick, r3, dp2)
        for j, add in enumerate(stencil(cy, mfy, next_col)):
            step = j - REACH
            if step < 0:
                add = jnp.where(col >= -step, add, 0.0)
            elif step > 0:
                add = jnp.where(col < COLS - step, add, 0.0)
            put(1, j, add, r2, dp1, r4, dp3)

        def weight(n, j, r):
            return weights[n, j, r + SIDE : r + SIDE + 1, :]

        def both(cells, n, r):
            total = weight(n, 0, r) * cells[0]
            for j in range(1, 7):
                total += weight(n, j, r) * cells[j]
            result = weight(n + 1, REACH, r) * total
            for j in range(7):
                if j != REACH:
                    shift = (REACH - j) % COLS
                    result += weight(n + 1, j, r) * pltpu.roll(total, shift, 1)
            return result

        def first(r):
            if r < 0:
                return jnp.where(odd, once[l, r + HALO], twice[l, r + HALO])
            if r >= ROWS:
                return jnp.where(odd, twice[l, r - ROWS], once[l, r - ROWS])
            return get_row(tracers, l, r)

        window = [first(r) for r in range(-HALO, 0)]
        for r in range(-REACH, ROWS + REACH):
            window.append(first(r + REACH))
            mid[r + REACH] = both(window, 0, r)
            window.pop(0)
        window = [mid[r] for r in range(HALO)]
        for r in range(ROWS):
            window.append(mid[r + HALO])
            done = both(window, 2, r)
            for h in range(2):
                out[row_of_all(l, r, h), :] = done[:, h * 128 : (h + 1) * 128]
            window.pop(0)
        return carry

    lax.fori_loop(0, LEV, level, 0)
    turned[...] = ends[...].T
    block = turned[pl.ds(pl.multiple_of(tracer * BLOCK, BLOCK), BLOCK), :]
    for l in range(LEV):
        start = l * SPAN + SIDE
        thick_out[l] = block[:, start : start + ROWS]


def shape(*dims):
    return jax.ShapeDtypeStruct(dims, jnp.float32)


def swap(block, start):
    count = lax.axis_size("space")
    pairs = [(i, i + 1) for i in range(start, count - 1, 2)]
    return lax.ppermute(block, "space", pairs + [(b, a) for a, b in pairs])


def per_device(tracers, thickness, wind_x, wind_y):
    count, steps = lax.axis_size("tracer"), lax.axis_size("space")
    turn = lambda x: jnp.transpose(x, (0, 2, 1))
    packed = pl.pallas_call(
        pack_fields,
        out_shape=shape(3, BLOCK, LEV * SPAN),
        in_specs=[pl.BlockSpec(memory_space=pl.ANY)] * 3,
        out_specs=VMEM,
        scratch_shapes=[
            pltpu.VMEM((3, LEV, BLOCK, ROWS), jnp.float32),
            pltpu.SemaphoreType.DMA((3,)),
        ],
    )(turn(thickness), turn(wind_x), turn(wind_y))
    same_chip = [[i, i + 1] for i in range(0, count, 2)]
    pair = lax.all_gather(packed, "tracer", axis_index_groups=same_chip)
    copies = pl.pallas_call(
        spread,
        out_shape=shape(count, 3 * BLOCK, LEV * SPAN),
        in_specs=[VMEM],
        out_specs=VMEM,
        compiler_params=PARAMS,
    )(pair)
    order = [(i + FIRST) % (count // 2) for i in range(count // 2)]
    members = [
        [
            (2 * j + core) * steps + (place + core) % steps
            for core in range(2)
            for j in order
        ]
        for place in range(steps)
    ]
    gathered = lax.all_to_all(
        copies, ("tracer", "space"), 0, 0, axis_index_groups=members
    )
    gathered = lax.all_gather(gathered, "tracer", axis_index_groups=same_chip)

    flat = tile_rows(tracers)
    once, twice = pl.pallas_call(
        pack_halos,
        out_shape=[shape(LEV, HALO, TR, COLS)] * 2,
        in_specs=[VMEM],
        out_specs=[VMEM] * 2,
        compiler_params=PARAMS,
    )(flat)
    once, twice = swap(once, 0), swap(twice, 1)

    values, thick = pl.pallas_call(
        sweeps,
        out_shape=[shape(TR * LEV * ROWS * 2, 128), shape(LEV, BLOCK, ROWS)],
        in_specs=[VMEM] * 4,
        out_specs=[VMEM] * 2,
        scratch_shapes=[
            pltpu.VMEM((3, LEV * SPAN, COLS), jnp.float32),
            pltpu.VMEM((ROWS + HALO, TR, COLS), jnp.float32),
            pltpu.VMEM((4, 7, SPAN, COLS), jnp.float32),
            pltpu.VMEM((LEV * SPAN, COLS), jnp.float32),
            pltpu.VMEM((COLS, LEV * SPAN), jnp.float32),
        ],
        compiler_params=PARAMS,
    )(gathered, flat, once, twice)
    return from_tile_rows(values), turn(thick)


def solution(mesh):
    in_specs = (
        P("tracer", None, "space", None),
        P(None, "space", "tracer"),
        P(None, "space", "tracer"),
        P(None, "space", "tracer"),
    )
    out_specs = (P("tracer", None, "space", None), P(None, "space", "tracer"))
    return jax.shard_map(
        per_device, mesh=mesh, in_specs=in_specs, out_specs=out_specs, check_vma=False
    )
```

```python
import jax
import jax.numpy as jnp
from jax import lax
from jax.experimental import pallas as pl
from jax.experimental.pallas import tpu as pltpu
from jax.sharding import PartitionSpec as P

COURANT_SCALE = 0.025
LEV, ROWS, COLS, TR = 4, 24, 256, 8
FIRST = 9
BLOCK = 8
REACH = 3
HALO = 2 * REACH
SIDE = 4
PART = 32
SHARE = 18
SPAN = ROWS + 2 * SIDE
VMEM = pl.BlockSpec(memory_space=pltpu.VMEM)
PARAMS = pltpu.CompilerParams(vmem_limit_bytes=24 * 1024 * 1024)


def pack_fields(thick, wind_x, wind_y, packed, held, arrived):
    copies = [
        pltpu.make_async_copy(field, held.at[f], arrived.at[f])
        for f, field in enumerate((thick, wind_x, wind_y))
    ]
    for copy in copies:
        copy.start()
    for copy in copies:
        copy.wait()
    whole = [jnp.concatenate([held[f, l] for l in range(LEV)], axis=1) for f in range(3)]
    ends = [
        [held[f, l][:, rows] for f in range(3) for l in range(LEV)]
        for rows in (slice(ROWS - SIDE, ROWS), slice(0, SIDE))
    ]
    for f in range(2):
        third = whole[2][:, f * PART : (f + 1) * PART]
        packed[f] = jnp.concatenate([whole[f], third], axis=1)
    packed[2] = jnp.concatenate([whole[2][:, 2 * PART :]] + ends[0] + ends[1], axis=1)


def spread(pair, copies):
    core = lax.axis_index("tracer") % 2
    lane = lax.broadcasted_iota(jnp.int32, (BLOCK, 128), 1)
    column = lax.broadcasted_iota(jnp.int32, (BLOCK, 128), 0)
    own = [jnp.where(core == 0, pair[0, n], pair[1, n]) for n in range(3)]
    rest = jnp.zeros((BLOCK, 128), jnp.float32)
    for n in range(4):
        moved = pltpu.roll(own[2], n * PART, 1) if n else own[2]
        mine = (lane >= n * PART) & (lane < (n + 1) * PART) & (column % 4 == n)
        rest = jnp.where(mine, moved, rest)
    rest = [jnp.sum(rest[4 * n : 4 * n + 4], axis=0, keepdims=True) for n in range(2)]
    first, second = pair[0, 2], pair[1, 2]
    last_rows = jnp.where(lane < 64, pltpu.roll(first, 96, 1), pltpu.roll(second, 32, 1))
    first_rows = jnp.where(lane < 64, pltpu.roll(second, 48, 1), pltpu.roll(first, 112, 1))
    beside = jnp.where(core == 0, last_rows, first_rows)
    half = copies.shape[0] // SHARE // 2
    for i in range(2 * half):
        at = SHARE * i
        same = core == 0 if i < half else core == 1
        copies[at : at + 8, :] = jnp.where(same, own[0], beside)
        copies[at + 8 : at + 16, :] = own[1]
        copies[at + 16 : at + 17, :] = rest[0]
        copies[at + 17 : at + 18, :] = rest[1]


def tile_rows(x):
    x = x.reshape(TR, LEV, ROWS // 8, 8, COLS // 128, 128)
    return jnp.transpose(x, (0, 1, 2, 4, 3, 5)).reshape(-1, 128)


def from_tile_rows(x):
    x = x.reshape(TR, LEV, ROWS // 8, COLS // 128, 8, 128)
    return jnp.transpose(x, (0, 1, 2, 4, 3, 5)).reshape(TR, LEV, ROWS, COLS)


def row_of_all(l, r, half):
    start = (l * (ROWS // 8) + r // 8) * (COLS // 128) * 8 + half * 8 + r % 8
    return pl.ds(start, TR, stride=LEV * ROWS * (COLS // 128))


def get_row(ref, l, r):
    return jnp.concatenate([ref[row_of_all(l, r, h), :] for h in range(2)], axis=1)


def pack_halos(tracers, once, twice):
    odd = lax.axis_index("space") % 2 == 1
    for l in range(LEV):
        for r in range(HALO):
            low = get_row(tracers, l, r)
            high = get_row(tracers, l, ROWS - HALO + r)
            once[l, r] = jnp.where(odd, low, high)
            twice[l, r] = jnp.where(odd, high, low)


def stencil(courant, flux, after):
    size = jnp.abs(courant)
    half = 0.5 * size
    curve = 3.0 * half * (1.0 - (2.0 / 3.0) * size)
    near = flux * (1.0 - half - curve)
    far = flux * (half - curve)
    mean = flux * (2.0 * curve)
    up = courant > 0
    far_l = jnp.where(up, far, 0.0)
    far_r = far - far_l
    mean_l = jnp.where(up, mean, 0.0)
    mean_r = mean - mean_l
    in_, out = 7.0 / 12.0, 1.0 / 12.0
    face = [
        -out * far_l,
        in_ * far_l - out * near,
        in_ * (far_l + near) - out * far_r + mean_l,
        in_ * (far_r + near) - out * far_l + mean_r,
        in_ * far_r - out * near,
        -out * far_r,
    ]
    moved = [after(w) for w in face]
    return (
        [face[0]]
        + [face[j] - moved[j - 1] for j in range(1, 6)]
        + [-moved[5]]
    )


def sweeps(
    gathered, tracers, once, twice, out, thick_out, fields, mid, weights, ends, turned
):
    space = lax.axis_index("space")
    tracer = lax.axis_index("tracer")
    last_row = lax.axis_size("space") * ROWS
    odd = space % 2 == 1
    half = gathered.shape[1] // SHARE // 2
    lane = lax.broadcasted_iota(jnp.int32, (BLOCK, 128), 1)
    column = lax.broadcasted_iota(jnp.int32, (BLOCK, 128), 0)
    blocks = [[], [], [], []]
    for chip in range(half):
        j = (chip - FIRST) % half
        hers = SHARE * (half + j)
        last_rows = gathered[1, SHARE * j : SHARE * j + 8, :]
        first_rows = gathered[0, hers : hers + 8, :]
        for core, at in ((0, SHARE * j), (1, hers)):
            blocks[0].append(gathered[core, at : at + 8, :])
            blocks[1].append(gathered[core, at + 8 : at + 16, :])
            rest = [gathered[core, at + 16 + n : at + 17 + n, :] for n in range(2)]
            blocks[2].append(jnp.where(column < 4, rest[0], rest[1]))
        blocks[3].append(jnp.where(lane < 64, last_rows, first_rows))
        blocks[3].append(jnp.where(lane < 64, first_rows, last_rows))
    turned_to = [jnp.concatenate(b, axis=0).T for b in blocks]
    col = lax.broadcasted_iota(jnp.int32, (PART, COLS), 1)
    rest = turned_to[2][:PART]
    for n in range(1, 4):
        rest = jnp.where(col % 4 == n, turned_to[2][n * PART : (n + 1) * PART], rest)
    whole = LEV * ROWS
    own = [turned_to[0][:whole], turned_to[1][:whole]]
    own.append(jnp.concatenate([turned_to[0][whole:], turned_to[1][whole:], rest], axis=0))
    size = 3 * LEV * SIDE
    col = lax.broadcasted_iota(jnp.int32, (size, COLS), 1)
    on_first = (col // BLOCK) % 2 == 0
    low_part, high_part = turned_to[3][:size], turned_to[3][64 : 64 + size]
    below = jnp.where(on_first, low_part, high_part)
    above = jnp.where(on_first, high_part, low_part)
    for f in range(3):
        for l in range(LEV):
            to, side = l * SPAN, (f * LEV + l) * SIDE
            for h in range(2):
                cut = slice(h * 128, (h + 1) * 128)
                fields[f, h, to : to + SIDE, :] = below[side : side + SIDE, cut]
                fields[f, h, to + SIDE : to + SIDE + ROWS, :] = own[f][
                    l * ROWS : (l + 1) * ROWS, cut
                ]
                fields[f, h, to + SIDE + ROWS : to + SPAN, :] = above[
                    side : side + SIDE, cut
                ]

    row = lax.broadcasted_iota(jnp.int32, (SPAN, COLS), 0) + (space * ROWS - SIDE)
    col = lax.broadcasted_iota(jnp.int32, (SPAN, COLS), 1)

    def level(l, carry):
        at = pl.ds(pl.multiple_of(l * SPAN, SPAN), SPAN)
        field = lambda f: jnp.concatenate([fields[f, h, at, :] for h in range(2)], axis=1)
        inside = (row >= 0) & (row < last_row)
        thick = jnp.where(inside, field(0), 1.0)
        next_row = lambda x: pltpu.roll(x, SPAN - 1, 0)
        next_col = lambda x: pltpu.roll(x, COLS - 1, 1)

        cx = jnp.where((row > 0) & (row < last_row), COURANT_SCALE * field(1), 0.0)
        mfx = cx * jnp.where(cx > 0, pltpu.roll(thick, 1, 0), thick)
        cy = jnp.where(inside & (col > 0), COURANT_SCALE * field(2), 0.0)
        mfy = cy * jnp.where(cy > 0, pltpu.roll(thick, 1, 1), thick)
        thin_x = next_row(mfx) - mfx
        thin_y = next_col(mfy) - mfy
        dp1 = thick - thin_x
        dp2 = dp1 - thin_y
        dp3 = dp2 - thin_x
        dp4 = dp3 - thin_y
        ends[at, :] = dp4
        r1, r2, r3, r4 = 1.0 / dp1, 1.0 / dp2, 1.0 / dp3, 1.0 / dp4

        def put(n, j, add, r_a, dp_a, r_b, dp_b):
            if j == 3:
                weights[n, j] = (add + dp_a) * r_a
                weights[n + 2, j] = (add + dp_b) * r_b
            else:
                weights[n, j] = add * r_a
                weights[n + 2, j] = add * r_b

        for j, add in enumerate(stencil(cx, mfx, next_row)):
            put(0, j, add, r1, thick, r3, dp2)
        for j, add in enumerate(stencil(cy, mfy, next_col)):
            step = j - REACH
            if step < 0:
                add = jnp.where(col >= -step, add, 0.0)
            elif step > 0:
                add = jnp.where(col < COLS - step, add, 0.0)
            put(1, j, add, r2, dp1, r4, dp3)

        def weight(n, j, r):
            return weights[n, j, r + SIDE : r + SIDE + 1, :]

        def both(cells, n, r):
            total = weight(n, 0, r) * cells[0]
            for j in range(1, 7):
                total += weight(n, j, r) * cells[j]
            result = weight(n + 1, REACH, r) * total
            for j in range(7):
                if j != REACH:
                    shift = (REACH - j) % COLS
                    result += weight(n + 1, j, r) * pltpu.roll(total, shift, 1)
            return result

        def first(r):
            if r < 0:
                return jnp.where(odd, once[l, r + HALO], twice[l, r + HALO])
            if r >= ROWS:
                return jnp.where(odd, twice[l, r - ROWS], once[l, r - ROWS])
            return get_row(tracers, l, r)

        window = [first(r) for r in range(-HALO, 0)]
        for r in range(-REACH, ROWS + REACH):
            window.append(first(r + REACH))
            mid[r + REACH] = both(window, 0, r)
            window.pop(0)
        window = [mid[r] for r in range(HALO)]
        for r in range(ROWS):
            window.append(mid[r + HALO])
            done = both(window, 2, r)
            for h in range(2):
                out[row_of_all(l, r, h), :] = done[:, h * 128 : (h + 1) * 128]
            window.pop(0)
        return carry

    lax.fori_loop(0, LEV, level, 0)
    turned[...] = ends[...].T
    block = turned[pl.ds(pl.multiple_of(tracer * BLOCK, BLOCK), BLOCK), :]
    for l in range(LEV):
        start = l * SPAN + SIDE
        thick_out[l] = block[:, start : start + ROWS]


def shape(*dims):
    return jax.ShapeDtypeStruct(dims, jnp.float32)


def swap(block, start):
    count = lax.axis_size("space")
    pairs = [(i, i + 1) for i in range(start, count - 1, 2)]
    return lax.ppermute(block, "space", pairs + [(b, a) for a, b in pairs])


def per_device(tracers, thickness, wind_x, wind_y):
    count, steps = lax.axis_size("tracer"), lax.axis_size("space")
    turn = lambda x: jnp.transpose(x, (0, 2, 1))
    packed = pl.pallas_call(
        pack_fields,
        out_shape=shape(3, BLOCK, 128),
        in_specs=[pl.BlockSpec(memory_space=pl.ANY)] * 3,
        out_specs=VMEM,
        scratch_shapes=[
            pltpu.VMEM((3, LEV, BLOCK, ROWS), jnp.float32),
            pltpu.SemaphoreType.DMA((3,)),
        ],
    )(turn(thickness), turn(wind_x), turn(wind_y))
    same_chip = [[i, i + 1] for i in range(0, count, 2)]
    pair = lax.all_gather(packed, "tracer", axis_index_groups=same_chip)
    copies = pl.pallas_call(
        spread,
        out_shape=shape(count * SHARE, 128),
        in_specs=[VMEM],
        out_specs=VMEM,
        compiler_params=PARAMS,
    )(pair)
    order = [(i + FIRST) % (count // 2) for i in range(count // 2)]
    members = [
        [
            (2 * j + core) * steps + (place + core) % steps
            for core in range(2)
            for j in order
        ]
        for place in range(steps)
    ]
    gathered = lax.all_to_all(
        copies.reshape(count, 1, SHARE * 128),
        ("tracer", "space"),
        0,
        0,
        axis_index_groups=members,
    )
    gathered = lax.all_gather(gathered, "tracer", axis_index_groups=same_chip)
    gathered = gathered.reshape(2, count * SHARE, 128)

    flat = tile_rows(tracers)
    once, twice = pl.pallas_call(
        pack_halos,
        out_shape=[shape(LEV, HALO, TR, COLS)] * 2,
        in_specs=[VMEM],
        out_specs=[VMEM] * 2,
        compiler_params=PARAMS,
    )(flat)
    once, twice = swap(once, 0), swap(twice, 1)

    values, thick = pl.pallas_call(
        sweeps,
        out_shape=[shape(TR * LEV * ROWS * 2, 128), shape(LEV, BLOCK, ROWS)],
        in_specs=[VMEM] * 4,
        out_specs=[VMEM] * 2,
        scratch_shapes=[
            pltpu.VMEM((3, 2, LEV * SPAN, 128), jnp.float32),
            pltpu.VMEM((ROWS + HALO, TR, COLS), jnp.float32),
            pltpu.VMEM((4, 7, SPAN, COLS), jnp.float32),
            pltpu.VMEM((LEV * SPAN, COLS), jnp.float32),
            pltpu.VMEM((COLS, LEV * SPAN), jnp.float32),
        ],
        compiler_params=PARAMS,
    )(gathered, flat, once, twice)
    return from_tile_rows(values), turn(thick)


def solution(mesh):
    in_specs = (
        P("tracer", None, "space", None),
        P(None, "space", "tracer"),
        P(None, "space", "tracer"),
        P(None, "space", "tracer"),
    )
    out_specs = (P("tracer", None, "space", None), P(None, "space", "tracer"))
    return jax.shard_map(
        per_device, mesh=mesh, in_specs=in_specs, out_specs=out_specs, check_vma=False
    )
```

```python
import jax
import jax.numpy as jnp
from jax import lax
from jax.experimental import pallas as pl
from jax.experimental.pallas import tpu as pltpu
from jax.sharding import PartitionSpec as P

COURANT_SCALE = 0.025
SUBSTEPS = 2
LEV, ROWS, COLS, TR = 4, 24, 256, 8
LEAD = 1
FIRST = 11
BLOCK = 8
REACH = 3
HALO = 2 * REACH
SIDE = 4
PART = 32
SHARE = 18
SPAN = ROWS + 2 * SIDE
VMEM = pl.BlockSpec(memory_space=pltpu.VMEM)
PARAMS = pltpu.CompilerParams(vmem_limit_bytes=24 * 1024 * 1024)


def packed(fields):
    whole = [jnp.concatenate([fields[f, l] for l in range(LEV)], axis=1) for f in range(3)]
    ends = [
        [fields[f, l][:, rows] for f in range(3) for l in range(LEV)]
        for rows in (slice(ROWS - SIDE, ROWS), slice(0, SIDE))
    ]
    thirds = [whole[2][:, n * PART : (n + 1) * PART] for n in range(3)]
    return [
        jnp.concatenate([whole[0], thirds[0]], axis=1),
        jnp.concatenate([whole[1], thirds[1]], axis=1),
        jnp.concatenate([thirds[2]] + ends[0] + ends[1], axis=1),
    ]


def spread(pair, copies):
    core = lax.axis_index("tracer") % 2
    lane = lax.broadcasted_iota(jnp.int32, (BLOCK, 128), 1)
    column = lax.broadcasted_iota(jnp.int32, (BLOCK, 128), 0)
    both = [packed(pair.at[n]) for n in range(2)]
    own = [jnp.where(core == 0, a, b) for a, b in zip(*both)]
    rest = jnp.zeros((BLOCK, 128), jnp.float32)
    for n in range(4):
        moved = pltpu.roll(own[2], n * PART, 1) if n else own[2]
        mine = (lane >= n * PART) & (lane < (n + 1) * PART) & (column % 4 == n)
        rest = jnp.where(mine, moved, rest)
    rest = [jnp.sum(rest[4 * n : 4 * n + 4], axis=0, keepdims=True) for n in range(2)]
    first, second = both[0][2], both[1][2]
    last_rows = jnp.where(lane < 64, pltpu.roll(first, 96, 1), pltpu.roll(second, 32, 1))
    first_rows = jnp.where(lane < 64, pltpu.roll(second, 48, 1), pltpu.roll(first, 112, 1))
    beside = jnp.where(core == 0, last_rows, first_rows)
    half = copies.shape[0] // SHARE // 2
    for i in range(2 * half):
        at = SHARE * i
        same = core == (LEAD if i < half else 1 - LEAD)
        copies[at : at + 8, :] = jnp.where(same, own[0], beside)
        copies[at + 8 : at + 16, :] = own[1]
        copies[at + 16 : at + 17, :] = rest[0]
        copies[at + 17 : at + 18, :] = rest[1]


def tile_rows(x):
    x = x.reshape(TR, LEV, ROWS // 8, 8, COLS // 128, 128)
    return jnp.transpose(x, (0, 1, 2, 4, 3, 5)).reshape(-1, 128)


def from_tile_rows(x):
    x = x.reshape(TR, LEV, ROWS // 8, COLS // 128, 8, 128)
    return jnp.transpose(x, (0, 1, 2, 4, 3, 5)).reshape(TR, LEV, ROWS, COLS)


def row_of_all(l, r, half):
    start = (l * (ROWS // 8) + r // 8) * (COLS // 128) * 8 + half * 8 + r % 8
    return pl.ds(start, TR, stride=LEV * ROWS * (COLS // 128))


def get_row(ref, l, r):
    return jnp.concatenate([ref[row_of_all(l, r, h), :] for h in range(2)], axis=1)


def pack_halos(tracers, once, twice):
    odd = lax.axis_index("space") % 2 == 1
    for l in range(LEV):
        for r in range(HALO):
            low = get_row(tracers, l, r)
            high = get_row(tracers, l, ROWS - HALO + r)
            once[l, r] = jnp.where(odd, low, high)
            twice[l, r] = jnp.where(odd, high, low)


def stencil(courant, flux, after):
    size = jnp.abs(courant)
    rest = 1.0 - size
    part = flux * rest * (1.0 / 12.0)
    near, far = part * rest, part * size
    mean = flux - 12.0 * (near - far)
    up = courant > 0
    far_l = jnp.where(up, far, 0.0)
    far_r = far - far_l
    mean_l = jnp.where(up, mean, 0.0)
    mean_r = mean - mean_l
    near7, left7, right7 = 7.0 * near, 7.0 * far_l, 7.0 * far_r
    outer_l, outer_r = left7 + near, right7 + near
    inner_l = (near7 - left7) + (far_r + mean_l)
    inner_r = (near7 - right7) + (far_l + mean_r)
    return [
        (far_l, 1),
        (outer_l + after(far_l), -1),
        (inner_l + after(outer_l), 1),
        (inner_r - after(inner_l), 1),
        (outer_r + after(inner_r), -1),
        (far_r + after(outer_r), 1),
        (after(far_r), -1),
    ]


def sweeps(
    gathered, tracers, once, twice, out, thick_out, fields, mid, weights, ends, turned
):
    space = lax.axis_index("space")
    tracer = lax.axis_index("tracer")
    last_row = lax.axis_size("space") * ROWS
    odd = space % 2 == 1
    half = gathered.shape[1] // SHARE // 2
    lane = lax.broadcasted_iota(jnp.int32, (BLOCK, 128), 1)
    column = lax.broadcasted_iota(jnp.int32, (BLOCK, 128), 0)
    blocks = [[], [], [], []]
    for chip in range(half):
        j = (chip - FIRST) % half
        places = [SHARE * (j + (0 if core == LEAD else half)) for core in range(2)]
        last_rows = gathered[1, places[0] : places[0] + 8, :]
        first_rows = gathered[0, places[1] : places[1] + 8, :]
        for core, at in enumerate(places):
            blocks[0].append(gathered[core, at : at + 8, :])
            blocks[1].append(gathered[core, at + 8 : at + 16, :])
            rest = [gathered[core, at + 16 + n : at + 17 + n, :] for n in range(2)]
            blocks[2].append(jnp.where(column < 4, rest[0], rest[1]))
        blocks[3].append(jnp.where(lane < 64, last_rows, first_rows))
        blocks[3].append(jnp.where(lane < 64, first_rows, last_rows))
    turned_to = [jnp.concatenate(b, axis=0).T for b in blocks]
    col = lax.broadcasted_iota(jnp.int32, (PART, COLS), 1)
    rest = turned_to[2][:PART]
    for n in range(1, 4):
        rest = jnp.where(col % 4 == n, turned_to[2][n * PART : (n + 1) * PART], rest)
    whole = LEV * ROWS
    own = [turned_to[0][:whole], turned_to[1][:whole]]
    own.append(jnp.concatenate([turned_to[0][whole:], turned_to[1][whole:], rest], axis=0))
    size = 3 * LEV * SIDE
    col = lax.broadcasted_iota(jnp.int32, (size, COLS), 1)
    on_first = (col // BLOCK) % 2 == 0
    low_part, high_part = turned_to[3][:size], turned_to[3][64 : 64 + size]
    below = jnp.where(on_first, low_part, high_part)
    above = jnp.where(on_first, high_part, low_part)
    for f in range(3):
        for l in range(LEV):
            to, side = l * SPAN, (f * LEV + l) * SIDE
            for h in range(2):
                cut = slice(h * 128, (h + 1) * 128)
                fields[f, h, to : to + SIDE, :] = below[side : side + SIDE, cut]
                fields[f, h, to + SIDE : to + SIDE + ROWS, :] = own[f][
                    l * ROWS : (l + 1) * ROWS, cut
                ]
                fields[f, h, to + SIDE + ROWS : to + SPAN, :] = above[
                    side : side + SIDE, cut
                ]

    row = lax.broadcasted_iota(jnp.int32, (SPAN, COLS), 0) + (space * ROWS - SIDE)
    col = lax.broadcasted_iota(jnp.int32, (SPAN, COLS), 1)

    def level(l, carry):
        at = pl.ds(pl.multiple_of(l * SPAN, SPAN), SPAN)
        field = lambda f: jnp.concatenate([fields[f, h, at, :] for h in range(2)], axis=1)
        inside = (row >= 0) & (row < last_row)
        thick = jnp.where(inside, field(0), 1.0)
        next_row = lambda x: pltpu.roll(x, SPAN - 1, 0)
        next_col = lambda x: pltpu.roll(x, COLS - 1, 1)

        cx = jnp.where((row > 0) & (row < last_row), COURANT_SCALE * field(1), 0.0)
        mfx = cx * jnp.where(cx > 0, pltpu.roll(thick, 1, 0), thick)
        cy = jnp.where(inside & (col > 0), COURANT_SCALE * field(2), 0.0)
        mfy = cy * jnp.where(cy > 0, pltpu.roll(thick, 1, 1), thick)
        thin_x = next_row(mfx) - mfx
        thin_y = next_col(mfy) - mfy
        dp1 = thick - thin_x
        dp2 = dp1 - thin_y
        dp3 = dp2 - thin_x
        dp4 = dp3 - thin_y
        ends[at, :] = dp4
        def put(n, adds, starts, results, placed):
            for substep in range(SUBSTEPS):
                over = 1.0 / results[substep]
                signed = {1: over, -1: -over}
                for j, (add, sign) in enumerate(adds):
                    if j == REACH:
                        add = add + starts[substep]
                    weights[2 * substep + n, j] = placed(j - REACH, add * signed[sign])

        def inside_only(adds):
            for j, (add, sign) in enumerate(adds):
                step = j - REACH
                if step < 0:
                    add = jnp.where(col >= -step, add, 0.0)
                elif step > 0:
                    add = jnp.where(col < COLS - step, add, 0.0)
                yield add, sign

        def placed(step, value):
            if abs(step) > 1:
                value = pltpu.roll(value, REACH if step > 0 else COLS - REACH, 1)
            return value

        put(0, stencil(cx, mfx, next_row), (thick, dp2), (dp1, dp3), lambda _, x: x)
        y_adds = list(inside_only(stencil(cy, mfy, next_col)))
        put(1, y_adds, (dp1, dp3), (dp2, dp4), placed)

        def weight(n, j, r):
            return weights[n, j, r + SIDE : r + SIDE + 1, :]

        def along(cells, substep, r):
            total = weight(2 * substep, 0, r) * cells[0]
            for j in range(1, 2 * REACH + 1):
                total += weight(2 * substep, j, r) * cells[j]
            return total

        def begin(q, substep, r):
            w = lambda j: weight(2 * substep + 1, j, r)
            left, right = pltpu.roll(q, 1, 1), next_col(q)
            up = w(0) * q + w(1) * right
            down = w(6) * q + w(5) * left
            return w(3) * q + w(2) * left + w(4) * right, up, down

        def end(total, up, down):
            return total + (pltpu.roll(up, REACH, 1) + pltpu.roll(down, COLS - REACH, 1))

        def first(r):
            if r < 0:
                return jnp.where(odd, once[l, r + HALO], twice[l, r + HALO])
            if r >= ROWS:
                return jnp.where(odd, twice[l, r - ROWS], once[l, r - ROWS])
            return get_row(tracers, l, r)

        def staged(rows, start, stages):
            rows = list(rows)
            held = [dict() for _ in stages]
            for n in range(len(rows) + 14 * (len(stages) - 1)):
                for k, stage in enumerate(stages):
                    at = n - 14 * k
                    if 0 <= at < len(rows):
                        args = held[k - 1].pop(at) if k else start(rows[at])
                        held[k][at] = stage(rows[at], *args)

        def keep_mid(r, *parts):
            mid[r + REACH] = end(*parts)

        def keep_out(r, *parts):
            done = end(*parts)
            for h in range(2):
                out[row_of_all(l, r, h), :] = done[:, h * 128 : (h + 1) * 128]

        window = [first(r) for r in range(-HALO, 0)]

        def next_first(r):
            window.append(first(r + REACH))
            return (list(window[-7:]),)

        staged(
            range(-REACH, ROWS + REACH),
            next_first,
            [
                lambda r, cells: (along(cells, 0, r),),
                lambda r, q: begin(q, 0, r),
                keep_mid,
            ],
        )
        window = [mid[r] for r in range(HALO)]

        def next_mid(r):
            window.append(mid[r + HALO])
            return (list(window[-7:]),)

        staged(
            range(ROWS),
            next_mid,
            [
                lambda r, cells: (along(cells, 1, r),),
                lambda r, q: begin(q, 1, r),
                keep_out,
            ],
        )
        return carry

    lax.fori_loop(0, LEV, level, 0)
    turned[...] = ends[...].T
    block = turned[pl.ds(pl.multiple_of(tracer * BLOCK, BLOCK), BLOCK), :]
    for l in range(LEV):
        start = l * SPAN + SIDE
        thick_out[l] = block[:, start : start + ROWS]


def shape(*dims):
    return jax.ShapeDtypeStruct(dims, jnp.float32)


def swap(block, start):
    count = lax.axis_size("space")
    pairs = [(i, i + 1) for i in range(start, count - 1, 2)]
    return lax.ppermute(block, "space", pairs + [(b, a) for a, b in pairs])


def per_device(tracers, thickness, wind_x, wind_y):
    count, steps = lax.axis_size("tracer"), lax.axis_size("space")
    turn = lambda x: jnp.transpose(x, (0, 2, 1))
    fields = jnp.stack([turn(thickness), turn(wind_x), turn(wind_y)])
    same_chip = [[i, i + 1] for i in range(0, count, 2)]
    pair = lax.all_gather(fields, "tracer", axis_index_groups=same_chip)
    copies = pl.pallas_call(
        spread,
        out_shape=shape(count * SHARE, 128),
        in_specs=[VMEM],
        out_specs=VMEM,
        compiler_params=PARAMS,
    )(pair)
    order = [(i + FIRST) % (count // 2) for i in range(count // 2)]
    members = [
        [
            (2 * j + core) * steps + (place + core) % steps
            for core in (LEAD, 1 - LEAD)
            for j in order
        ]
        for place in range(steps)
    ]
    gathered = lax.all_to_all(
        copies.reshape(count, 1, SHARE * 128),
        ("tracer", "space"),
        0,
        0,
        axis_index_groups=members,
    )
    gathered = lax.all_gather(gathered, "tracer", axis_index_groups=same_chip)
    gathered = gathered.reshape(2, count * SHARE, 128)

    flat = tile_rows(tracers)
    once, twice = pl.pallas_call(
        pack_halos,
        out_shape=[shape(LEV, HALO, TR, COLS)] * 2,
        in_specs=[VMEM],
        out_specs=[VMEM] * 2,
        compiler_params=PARAMS,
    )(flat)
    once, twice = swap(once, 0), swap(twice, 1)

    values, thick = pl.pallas_call(
        sweeps,
        out_shape=[shape(TR * LEV * ROWS * 2, 128), shape(LEV, BLOCK, ROWS)],
        in_specs=[VMEM] * 4,
        out_specs=[VMEM] * 2,
        scratch_shapes=[
            pltpu.VMEM((3, 2, LEV * SPAN, 128), jnp.float32),
            pltpu.VMEM((ROWS + HALO, TR, COLS), jnp.float32),
            pltpu.VMEM((4, 7, SPAN, COLS), jnp.float32),
            pltpu.VMEM((LEV * SPAN, COLS), jnp.float32),
            pltpu.VMEM((COLS, LEV * SPAN), jnp.float32),
        ],
        compiler_params=PARAMS,
    )(gathered, flat, once, twice)
    return from_tile_rows(values), turn(thick)


def solution(mesh):
    in_specs = (
        P("tracer", None, "space", None),
        P(None, "space", "tracer"),
        P(None, "space", "tracer"),
        P(None, "space", "tracer"),
    )
    out_specs = (P("tracer", None, "space", None), P(None, "space", "tracer"))
    return jax.shard_map(
        per_device, mesh=mesh, in_specs=in_specs, out_specs=out_specs, check_vma=False
    )
```

```python
import jax
import jax.numpy as jnp
from jax import lax
from jax.experimental import pallas as pl
from jax.experimental.pallas import tpu as pltpu
from jax.sharding import PartitionSpec as P

COURANT_SCALE = 0.025
SUBSTEPS = 2
LEV, ROWS, COLS, TR = 4, 24, 256, 8
LEAD = 1
FIRST = 11
BLOCK = 8
REACH = 3
HALO = 2 * REACH
SIDE = 4
PART = 32
SHARE = 18
SPAN = ROWS + 2 * SIDE
VMEM = pl.BlockSpec(memory_space=pltpu.VMEM)
PARAMS = pltpu.CompilerParams(vmem_limit_bytes=24 * 1024 * 1024)


def listed(chips):
    return [(i + FIRST) % chips for i in range(chips)]


def packed(fields):
    whole = [jnp.concatenate([fields[f, l] for l in range(LEV)], axis=1) for f in range(3)]
    ends = [
        [fields[f, l][:, rows] for f in range(3) for l in range(LEV)]
        for rows in (slice(ROWS - SIDE, ROWS), slice(0, SIDE))
    ]
    thirds = [whole[2][:, n * PART : (n + 1) * PART] for n in range(3)]
    return [
        jnp.concatenate([whole[0], thirds[0]], axis=1),
        jnp.concatenate([whole[1], thirds[1]], axis=1),
        jnp.concatenate([thirds[2]] + ends[0] + ends[1], axis=1),
    ]


def spread(pair, copies):
    core = lax.axis_index("tracer") % 2
    lane = lax.broadcasted_iota(jnp.int32, (BLOCK, 128), 1)
    column = lax.broadcasted_iota(jnp.int32, (BLOCK, 128), 0)
    both = [packed(pair.at[n]) for n in range(2)]
    own = [jnp.where(core == 0, a, b) for a, b in zip(*both)]
    rest = jnp.zeros((BLOCK, 128), jnp.float32)
    for n in range(4):
        moved = pltpu.roll(own[2], n * PART, 1) if n else own[2]
        mine = (lane >= n * PART) & (lane < (n + 1) * PART) & (column % 4 == n)
        rest = jnp.where(mine, moved, rest)
    rest = [jnp.sum(rest[4 * n : 4 * n + 4], axis=0, keepdims=True) for n in range(2)]
    first, second = both[0][2], both[1][2]
    last_rows = jnp.where(lane < 64, pltpu.roll(first, 96, 1), pltpu.roll(second, 32, 1))
    first_rows = jnp.where(lane < 64, pltpu.roll(second, 48, 1), pltpu.roll(first, 112, 1))
    beside = jnp.where(core == 0, last_rows, first_rows)
    half = copies.shape[0] // SHARE // 2
    for i in range(2 * half):
        at = SHARE * i
        same = core == (LEAD if i % 2 == 0 else 1 - LEAD)
        copies[at : at + 8, :] = jnp.where(same, own[0], beside)
        copies[at + 8 : at + 16, :] = own[1]
        copies[at + 16 : at + 17, :] = rest[0]
        copies[at + 17 : at + 18, :] = rest[1]


def tile_rows(x):
    x = x.reshape(TR, LEV, ROWS // 8, 8, COLS // 128, 128)
    return jnp.transpose(x, (0, 1, 2, 4, 3, 5)).reshape(-1, 128)


def from_tile_rows(x):
    x = x.reshape(TR, LEV, ROWS // 8, COLS // 128, 8, 128)
    return jnp.transpose(x, (0, 1, 2, 4, 3, 5)).reshape(TR, LEV, ROWS, COLS)


def row_of_all(l, r, half):
    start = (l * (ROWS // 8) + r // 8) * (COLS // 128) * 8 + half * 8 + r % 8
    return pl.ds(start, TR, stride=LEV * ROWS * (COLS // 128))


def get_row(ref, l, r):
    return jnp.concatenate([ref[row_of_all(l, r, h), :] for h in range(2)], axis=1)


def pack_halos(tracers, once, twice):
    odd = lax.axis_index("space") % 2 == 1
    for l in range(LEV):
        for r in range(HALO):
            low = get_row(tracers, l, r)
            high = get_row(tracers, l, ROWS - HALO + r)
            once[l, r] = jnp.where(odd, low, high)
            twice[l, r] = jnp.where(odd, high, low)


def stencil(courant, flux, after):
    size = jnp.abs(courant)
    rest = 1.0 - size
    part = flux * rest * (1.0 / 12.0)
    near, far = part * rest, part * size
    mean = flux - 12.0 * (near - far)
    up = courant > 0
    far_l = jnp.where(up, far, 0.0)
    far_r = far - far_l
    mean_l = jnp.where(up, mean, 0.0)
    mean_r = mean - mean_l
    near7, left7, right7 = 7.0 * near, 7.0 * far_l, 7.0 * far_r
    outer_l, outer_r = left7 + near, right7 + near
    inner_l = (near7 - left7) + (far_r + mean_l)
    inner_r = (near7 - right7) + (far_l + mean_r)
    return [
        (far_l, 1),
        (outer_l + after(far_l), -1),
        (inner_l + after(outer_l), 1),
        (inner_r - after(inner_l), 1),
        (outer_r + after(inner_r), -1),
        (far_r + after(outer_r), 1),
        (after(far_r), -1),
    ]


def sweeps(
    gathered, tracers, once, twice, out, thick_out, fields, mid, weights, ends, turned
):
    space = lax.axis_index("space")
    tracer = lax.axis_index("tracer")
    last_row = lax.axis_size("space") * ROWS
    odd = space % 2 == 1
    half = gathered.shape[1] // SHARE // 2
    lane = lax.broadcasted_iota(jnp.int32, (BLOCK, 128), 1)
    column = lax.broadcasted_iota(jnp.int32, (BLOCK, 128), 0)
    blocks = [[], [], [], []]
    for chip in range(half):
        j = listed(half).index(chip)
        places = [SHARE * (2 * j + (0 if core == LEAD else 1)) for core in range(2)]
        last_rows = gathered[1, places[0] : places[0] + 8, :]
        first_rows = gathered[0, places[1] : places[1] + 8, :]
        for core, at in enumerate(places):
            blocks[0].append(gathered[core, at : at + 8, :])
            blocks[1].append(gathered[core, at + 8 : at + 16, :])
            rest = [gathered[core, at + 16 + n : at + 17 + n, :] for n in range(2)]
            blocks[2].append(jnp.where(column < 4, rest[0], rest[1]))
        blocks[3].append(jnp.where(lane < 64, last_rows, first_rows))
        blocks[3].append(jnp.where(lane < 64, first_rows, last_rows))
    turned_to = [jnp.concatenate(b, axis=0).T for b in blocks]
    col = lax.broadcasted_iota(jnp.int32, (PART, COLS), 1)
    rest = turned_to[2][:PART]
    for n in range(1, 4):
        rest = jnp.where(col % 4 == n, turned_to[2][n * PART : (n + 1) * PART], rest)
    whole = LEV * ROWS
    own = [turned_to[0][:whole], turned_to[1][:whole]]
    own.append(jnp.concatenate([turned_to[0][whole:], turned_to[1][whole:], rest], axis=0))
    size = 3 * LEV * SIDE
    col = lax.broadcasted_iota(jnp.int32, (size, COLS), 1)
    on_first = (col // BLOCK) % 2 == 0
    low_part, high_part = turned_to[3][:size], turned_to[3][64 : 64 + size]
    below = jnp.where(on_first, low_part, high_part)
    above = jnp.where(on_first, high_part, low_part)
    for f in range(3):
        for l in range(LEV):
            to, side = l * SPAN, (f * LEV + l) * SIDE
            for h in range(2):
                cut = slice(h * 128, (h + 1) * 128)
                fields[f, h, to : to + SIDE, :] = below[side : side + SIDE, cut]
                fields[f, h, to + SIDE : to + SIDE + ROWS, :] = own[f][
                    l * ROWS : (l + 1) * ROWS, cut
                ]
                fields[f, h, to + SIDE + ROWS : to + SPAN, :] = above[
                    side : side + SIDE, cut
                ]

    row = lax.broadcasted_iota(jnp.int32, (SPAN, COLS), 0) + (space * ROWS - SIDE)
    col = lax.broadcasted_iota(jnp.int32, (SPAN, COLS), 1)

    def level(l, carry):
        at = pl.ds(pl.multiple_of(l * SPAN, SPAN), SPAN)
        field = lambda f: jnp.concatenate([fields[f, h, at, :] for h in range(2)], axis=1)
        inside = (row >= 0) & (row < last_row)
        thick = jnp.where(inside, field(0), 1.0)
        next_row = lambda x: pltpu.roll(x, SPAN - 1, 0)
        next_col = lambda x: pltpu.roll(x, COLS - 1, 1)

        cx = jnp.where((row > 0) & (row < last_row), COURANT_SCALE * field(1), 0.0)
        mfx = cx * jnp.where(cx > 0, pltpu.roll(thick, 1, 0), thick)
        cy = jnp.where(inside & (col > 0), COURANT_SCALE * field(2), 0.0)
        mfy = cy * jnp.where(cy > 0, pltpu.roll(thick, 1, 1), thick)
        thin_x = next_row(mfx) - mfx
        thin_y = next_col(mfy) - mfy
        dp1 = thick - thin_x
        dp2 = dp1 - thin_y
        dp3 = dp2 - thin_x
        dp4 = dp3 - thin_y
        ends[at, :] = dp4
        def put(n, adds, starts, results, placed):
            for substep in range(SUBSTEPS):
                over = 1.0 / results[substep]
                signed = {1: over, -1: -over}
                for j, (add, sign) in enumerate(adds):
                    if j == REACH:
                        add = add + starts[substep]
                    weights[2 * substep + n, j] = placed(j - REACH, add * signed[sign])

        def inside_only(adds):
            for j, (add, sign) in enumerate(adds):
                step = j - REACH
                if step < 0:
                    add = jnp.where(col >= -step, add, 0.0)
                elif step > 0:
                    add = jnp.where(col < COLS - step, add, 0.0)
                yield add, sign

        def placed(step, value):
            if abs(step) > 1:
                value = pltpu.roll(value, REACH if step > 0 else COLS - REACH, 1)
            return value

        put(0, stencil(cx, mfx, next_row), (thick, dp2), (dp1, dp3), lambda _, x: x)
        y_adds = list(inside_only(stencil(cy, mfy, next_col)))
        put(1, y_adds, (dp1, dp3), (dp2, dp4), placed)

        def weight(n, j, r):
            return weights[n, j, r + SIDE : r + SIDE + 1, :]

        def along(cells, substep, r):
            total = weight(2 * substep, 0, r) * cells[0]
            for j in range(1, 2 * REACH + 1):
                total += weight(2 * substep, j, r) * cells[j]
            return total

        def begin(q, substep, r):
            w = lambda j: weight(2 * substep + 1, j, r)
            left, right = pltpu.roll(q, 1, 1), next_col(q)
            up = w(0) * q + w(1) * right
            down = w(6) * q + w(5) * left
            return w(3) * q + w(2) * left + w(4) * right, up, down

        def end(total, up, down):
            return total + (pltpu.roll(up, REACH, 1) + pltpu.roll(down, COLS - REACH, 1))

        def first(r):
            if r < 0:
                return jnp.where(odd, once[l, r + HALO], twice[l, r + HALO])
            if r >= ROWS:
                return jnp.where(odd, twice[l, r - ROWS], once[l, r - ROWS])
            return get_row(tracers, l, r)

        def staged(rows, start, stages):
            rows = list(rows)
            held = [dict() for _ in stages]
            for n in range(len(rows) + 14 * (len(stages) - 1)):
                for k, stage in enumerate(stages):
                    at = n - 14 * k
                    if 0 <= at < len(rows):
                        args = held[k - 1].pop(at) if k else start(rows[at])
                        held[k][at] = stage(rows[at], *args)

        def keep_mid(r, *parts):
            mid[r + REACH] = end(*parts)

        def keep_out(r, *parts):
            done = end(*parts)
            for h in range(2):
                out[row_of_all(l, r, h), :] = done[:, h * 128 : (h + 1) * 128]

        window = [first(r) for r in range(-HALO, 0)]

        def next_first(r):
            window.append(first(r + REACH))
            return (list(window[-7:]),)

        staged(
            range(-REACH, ROWS + REACH),
            next_first,
            [
                lambda r, cells: (along(cells, 0, r),),
                lambda r, q: begin(q, 0, r),
                keep_mid,
            ],
        )
        window = [mid[r] for r in range(HALO)]

        def next_mid(r):
            window.append(mid[r + HALO])
            return (list(window[-7:]),)

        staged(
            range(ROWS),
            next_mid,
            [
                lambda r, cells: (along(cells, 1, r),),
                lambda r, q: begin(q, 1, r),
                keep_out,
            ],
        )
        return carry

    lax.fori_loop(0, LEV, level, 0)
    turned[...] = ends[...].T
    block = turned[pl.ds(pl.multiple_of(tracer * BLOCK, BLOCK), BLOCK), :]
    for l in range(LEV):
        start = l * SPAN + SIDE
        thick_out[l] = block[:, start : start + ROWS]


def shape(*dims):
    return jax.ShapeDtypeStruct(dims, jnp.float32)


def swap(block, start):
    count = lax.axis_size("space")
    pairs = [(i, i + 1) for i in range(start, count - 1, 2)]
    return lax.ppermute(block, "space", pairs + [(b, a) for a, b in pairs])


def per_device(tracers, thickness, wind_x, wind_y):
    count, steps = lax.axis_size("tracer"), lax.axis_size("space")
    turn = lambda x: jnp.transpose(x, (0, 2, 1))
    fields = jnp.stack([turn(thickness), turn(wind_x), turn(wind_y)])
    same_chip = [[i, i + 1] for i in range(0, count, 2)]
    pair = lax.all_gather(fields, "tracer", axis_index_groups=same_chip)
    copies = pl.pallas_call(
        spread,
        out_shape=shape(count * SHARE, 128),
        in_specs=[VMEM],
        out_specs=VMEM,
        compiler_params=PARAMS,
    )(pair)
    order = listed(count // 2)
    members = [
        [
            (2 * j + core) * steps + (place + core) % steps
            for j in order
            for core in (LEAD, 1 - LEAD)
        ]
        for place in range(steps)
    ]
    gathered = lax.all_to_all(
        copies.reshape(count, 1, SHARE * 128),
        ("tracer", "space"),
        0,
        0,
        axis_index_groups=members,
    )
    gathered = lax.all_gather(gathered, "tracer", axis_index_groups=same_chip)
    gathered = gathered.reshape(2, count * SHARE, 128)

    flat = tile_rows(tracers)
    once, twice = pl.pallas_call(
        pack_halos,
        out_shape=[shape(LEV, HALO, TR, COLS)] * 2,
        in_specs=[VMEM],
        out_specs=[VMEM] * 2,
        compiler_params=PARAMS,
    )(flat)
    once, twice = swap(once, 0), swap(twice, 1)

    values, thick = pl.pallas_call(
        sweeps,
        out_shape=[shape(TR * LEV * ROWS * 2, 128), shape(LEV, BLOCK, ROWS)],
        in_specs=[VMEM] * 4,
        out_specs=[VMEM] * 2,
        scratch_shapes=[
            pltpu.VMEM((3, 2, LEV * SPAN, 128), jnp.float32),
            pltpu.VMEM((ROWS + HALO, TR, COLS), jnp.float32),
            pltpu.VMEM((4, 7, SPAN, COLS), jnp.float32),
            pltpu.VMEM((LEV * SPAN, COLS), jnp.float32),
            pltpu.VMEM((COLS, LEV * SPAN), jnp.float32),
        ],
        compiler_params=PARAMS,
    )(gathered, flat, once, twice)
    return from_tile_rows(values), turn(thick)


def solution(mesh):
    in_specs = (
        P("tracer", None, "space", None),
        P(None, "space", "tracer"),
        P(None, "space", "tracer"),
        P(None, "space", "tracer"),
    )
    out_specs = (P("tracer", None, "space", None), P(None, "space", "tracer"))
    return jax.shard_map(
        per_device, mesh=mesh, in_specs=in_specs, out_specs=out_specs, check_vma=False
    )
```

```python
import jax
import jax.numpy as jnp
from jax import lax
from jax.experimental import pallas as pl
from jax.experimental.pallas import tpu as pltpu
from jax.sharding import PartitionSpec as P

COURANT_SCALE = 0.025
SUBSTEPS = 2
LEV, ROWS, COLS, TR = 4, 24, 256, 8
LEAD = 1
FIRST = 11
BLOCK = 8
REACH = 3
HALO = 2 * REACH
SIDE = 4
PART = 32
SHARE = 18
SPAN = ROWS + 2 * SIDE
VMEM = pl.BlockSpec(memory_space=pltpu.VMEM)
PARAMS = pltpu.CompilerParams(vmem_limit_bytes=24 * 1024 * 1024)


def listed(chips):
    return [(i + FIRST) % chips for i in range(chips)]


def packed(fields):
    whole = [jnp.concatenate([fields[f, l] for l in range(LEV)], axis=1) for f in range(3)]
    ends = [
        [fields[f, l][:, rows] for f in range(3) for l in range(LEV)]
        for rows in (slice(ROWS - SIDE, ROWS), slice(0, SIDE))
    ]
    thirds = [whole[2][:, n * PART : (n + 1) * PART] for n in range(3)]
    return [
        jnp.concatenate([whole[0], thirds[0]], axis=1),
        jnp.concatenate([whole[1], thirds[1]], axis=1),
        jnp.concatenate([thirds[2]] + ends[0] + ends[1], axis=1),
    ]


def spread(pair, copies):
    core = lax.axis_index("tracer") % 2
    lane = lax.broadcasted_iota(jnp.int32, (BLOCK, 128), 1)
    column = lax.broadcasted_iota(jnp.int32, (BLOCK, 128), 0)
    both = [packed(pair.at[n]) for n in range(2)]
    own = [jnp.where(core == 0, a, b) for a, b in zip(*both)]
    rest = jnp.zeros((BLOCK, 128), jnp.float32)
    for n in range(4):
        moved = pltpu.roll(own[2], n * PART, 1) if n else own[2]
        mine = (lane >= n * PART) & (lane < (n + 1) * PART) & (column % 4 == n)
        rest = jnp.where(mine, moved, rest)
    rest = [jnp.sum(rest[4 * n : 4 * n + 4], axis=0, keepdims=True) for n in range(2)]
    first, second = both[0][2], both[1][2]
    last_rows = jnp.where(lane < 64, pltpu.roll(first, 96, 1), pltpu.roll(second, 32, 1))
    first_rows = jnp.where(lane < 64, pltpu.roll(second, 48, 1), pltpu.roll(first, 112, 1))
    beside = jnp.where(core == 0, last_rows, first_rows)
    half = copies.shape[0] // SHARE // 2
    for i in range(2 * half):
        at = SHARE * i
        same = core == (LEAD if i % 2 == 0 else 1 - LEAD)
        copies[at : at + 8, :] = jnp.where(same, own[0], beside)
        copies[at + 8 : at + 16, :] = own[1]
        copies[at + 16 : at + 17, :] = rest[0]
        copies[at + 17 : at + 18, :] = rest[1]


def tile_rows(x):
    x = x.reshape(TR, LEV, ROWS // 8, 8, COLS // 128, 128)
    return jnp.transpose(x, (0, 1, 2, 4, 3, 5)).reshape(-1, 128)


def from_tile_rows(x):
    x = x.reshape(TR, LEV, ROWS // 8, COLS // 128, 8, 128)
    return jnp.transpose(x, (0, 1, 2, 4, 3, 5)).reshape(TR, LEV, ROWS, COLS)


def row_of_all(l, r, half):
    start = (l * (ROWS // 8) + r // 8) * (COLS // 128) * 8 + half * 8 + r % 8
    return pl.ds(start, TR, stride=LEV * ROWS * (COLS // 128))


def get_row(ref, l, r):
    return jnp.concatenate([ref[row_of_all(l, r, h), :] for h in range(2)], axis=1)


def pack_halos(tracers, once, twice):
    odd = lax.axis_index("space") % 2 == 1
    for l in range(LEV):
        for r in range(HALO):
            low = get_row(tracers, l, r)
            high = get_row(tracers, l, ROWS - HALO + r)
            once[l, r] = jnp.where(odd, low, high)
            twice[l, r] = jnp.where(odd, high, low)


def stencil(courant, flux, after):
    size = jnp.abs(courant)
    rest = 1.0 - size
    part = flux * rest * (1.0 / 12.0)
    near, far = part * rest, part * size
    mean = flux - 12.0 * (near - far)
    up = courant > 0
    far_l = jnp.where(up, far, 0.0)
    far_r = far - far_l
    mean_l = jnp.where(up, mean, 0.0)
    mean_r = mean - mean_l
    near7, left7, right7 = 7.0 * near, 7.0 * far_l, 7.0 * far_r
    outer_l, outer_r = left7 + near, right7 + near
    inner_l = (near7 - left7) + (far_r + mean_l)
    inner_r = (near7 - right7) + (far_l + mean_r)
    return [
        (far_l, 1),
        (outer_l + after(far_l), -1),
        (inner_l + after(outer_l), 1),
        (inner_r - after(inner_l), 1),
        (outer_r + after(inner_r), -1),
        (far_r + after(outer_r), 1),
        (after(far_r), -1),
    ]


def sweeps(
    gathered, tracers, twice, once, out, thick_out, fields, mid, weights, ends, turned
):
    space = lax.axis_index("space")
    tracer = lax.axis_index("tracer")
    last_row = lax.axis_size("space") * ROWS
    odd = space % 2 == 1
    half = gathered.shape[1] // SHARE // 2
    lane = lax.broadcasted_iota(jnp.int32, (BLOCK, 128), 1)
    column = lax.broadcasted_iota(jnp.int32, (BLOCK, 128), 0)
    blocks = [[], [], [], []]
    for chip in range(half):
        j = listed(half).index(chip)
        places = [SHARE * (2 * j + (0 if core == LEAD else 1)) for core in range(2)]
        last_rows = gathered[1, places[0] : places[0] + 8, :]
        first_rows = gathered[0, places[1] : places[1] + 8, :]
        for core, at in enumerate(places):
            blocks[0].append(gathered[core, at : at + 8, :])
            blocks[1].append(gathered[core, at + 8 : at + 16, :])
            rest = [gathered[core, at + 16 + n : at + 17 + n, :] for n in range(2)]
            blocks[2].append(jnp.where(column < 4, rest[0], rest[1]))
        blocks[3].append(jnp.where(lane < 64, last_rows, first_rows))
        blocks[3].append(jnp.where(lane < 64, first_rows, last_rows))
    turned_to = [jnp.concatenate(b, axis=0).T for b in blocks]
    col = lax.broadcasted_iota(jnp.int32, (PART, COLS), 1)
    rest = turned_to[2][:PART]
    for n in range(1, 4):
        rest = jnp.where(col % 4 == n, turned_to[2][n * PART : (n + 1) * PART], rest)
    whole = LEV * ROWS
    own = [turned_to[0][:whole], turned_to[1][:whole]]
    own.append(jnp.concatenate([turned_to[0][whole:], turned_to[1][whole:], rest], axis=0))
    size = 3 * LEV * SIDE
    col = lax.broadcasted_iota(jnp.int32, (size, COLS), 1)
    on_first = (col // BLOCK) % 2 == 0
    low_part, high_part = turned_to[3][:size], turned_to[3][64 : 64 + size]
    below = jnp.where(on_first, low_part, high_part)
    above = jnp.where(on_first, high_part, low_part)
    for f in range(3):
        for l in range(LEV):
            to, side = l * SPAN, (f * LEV + l) * SIDE
            for h in range(2):
                cut = slice(h * 128, (h + 1) * 128)
                fields[f, h, to : to + SIDE, :] = below[side : side + SIDE, cut]
                fields[f, h, to + SIDE : to + SIDE + ROWS, :] = own[f][
                    l * ROWS : (l + 1) * ROWS, cut
                ]
                fields[f, h, to + SIDE + ROWS : to + SPAN, :] = above[
                    side : side + SIDE, cut
                ]

    row = lax.broadcasted_iota(jnp.int32, (SPAN, COLS), 0) + (space * ROWS - SIDE)
    col = lax.broadcasted_iota(jnp.int32, (SPAN, COLS), 1)

    def level(l, carry):
        at = pl.ds(pl.multiple_of(l * SPAN, SPAN), SPAN)
        field = lambda f: jnp.concatenate([fields[f, h, at, :] for h in range(2)], axis=1)
        inside = (row >= 0) & (row < last_row)
        thick = jnp.where(inside, field(0), 1.0)
        next_row = lambda x: pltpu.roll(x, SPAN - 1, 0)
        next_col = lambda x: pltpu.roll(x, COLS - 1, 1)

        cx = jnp.where((row > 0) & (row < last_row), COURANT_SCALE * field(1), 0.0)
        mfx = cx * jnp.where(cx > 0, pltpu.roll(thick, 1, 0), thick)
        cy = jnp.where(inside & (col > 0), COURANT_SCALE * field(2), 0.0)
        mfy = cy * jnp.where(cy > 0, pltpu.roll(thick, 1, 1), thick)
        thin_x = next_row(mfx) - mfx
        thin_y = next_col(mfy) - mfy
        dp1 = thick - thin_x
        dp2 = dp1 - thin_y
        dp3 = dp2 - thin_x
        dp4 = dp3 - thin_y
        ends[at, :] = dp4
        def put(n, adds, starts, results, placed):
            for substep in range(SUBSTEPS):
                over = 1.0 / results[substep]
                signed = {1: over, -1: -over}
                for j, (add, sign) in enumerate(adds):
                    if j == REACH:
                        add = add + starts[substep]
                    weights[2 * substep + n, j] = placed(j - REACH, add * signed[sign])

        def inside_only(adds):
            for j, (add, sign) in enumerate(adds):
                step = j - REACH
                if step < 0:
                    add = jnp.where(col >= -step, add, 0.0)
                elif step > 0:
                    add = jnp.where(col < COLS - step, add, 0.0)
                yield add, sign

        def placed(step, value):
            if abs(step) > 1:
                value = pltpu.roll(value, REACH if step > 0 else COLS - REACH, 1)
            return value

        put(0, stencil(cx, mfx, next_row), (thick, dp2), (dp1, dp3), lambda _, x: x)
        y_adds = list(inside_only(stencil(cy, mfy, next_col)))
        put(1, y_adds, (dp1, dp3), (dp2, dp4), placed)

        def weight(n, j, r):
            return weights[n, j, r + SIDE : r + SIDE + 1, :]

        def along(cells, substep, r):
            total = weight(2 * substep, 0, r) * cells[0]
            for j in range(1, 2 * REACH + 1):
                total += weight(2 * substep, j, r) * cells[j]
            return total

        def begin(q, substep, r):
            w = lambda j: weight(2 * substep + 1, j, r)
            left, right = pltpu.roll(q, 1, 1), next_col(q)
            up = w(0) * q + w(1) * right
            down = w(6) * q + w(5) * left
            return w(3) * q + w(2) * left + w(4) * right, up, down

        def end(total, up, down):
            return total + (pltpu.roll(up, REACH, 1) + pltpu.roll(down, COLS - REACH, 1))

        def first(r):
            if r < 0:
                return jnp.where(odd, once[l, r + HALO], twice[l, r + HALO])
            if r >= ROWS:
                return jnp.where(odd, twice[l, r - ROWS], once[l, r - ROWS])
            return get_row(tracers, l, r)

        def staged(rows, start, stages):
            rows = list(rows)
            held = [dict() for _ in stages]
            for n in range(len(rows) + 14 * (len(stages) - 1)):
                for k, stage in enumerate(stages):
                    at = n - 14 * k
                    if 0 <= at < len(rows):
                        args = held[k - 1].pop(at) if k else start(rows[at])
                        held[k][at] = stage(rows[at], *args)

        def keep_mid(r, *parts):
            mid[r + REACH] = end(*parts)

        def keep_out(r, *parts):
            done = end(*parts)
            for h in range(2):
                out[row_of_all(l, r, h), :] = done[:, h * 128 : (h + 1) * 128]

        window = [first(r) for r in range(-HALO, 0)]

        def next_first(r):
            window.append(first(r + REACH))
            return (list(window[-7:]),)

        staged(
            range(-REACH, ROWS + REACH),
            next_first,
            [
                lambda r, cells: (along(cells, 0, r),),
                lambda r, q: begin(q, 0, r),
                keep_mid,
            ],
        )
        window = [mid[r] for r in range(HALO)]

        def next_mid(r):
            window.append(mid[r + HALO])
            return (list(window[-7:]),)

        staged(
            range(ROWS),
            next_mid,
            [
                lambda r, cells: (along(cells, 1, r),),
                lambda r, q: begin(q, 1, r),
                keep_out,
            ],
        )
        return carry

    lax.fori_loop(0, LEV, level, 0)
    turned[...] = ends[...].T
    block = turned[pl.ds(pl.multiple_of(tracer * BLOCK, BLOCK), BLOCK), :]
    for l in range(LEV):
        start = l * SPAN + SIDE
        thick_out[l] = block[:, start : start + ROWS]


def shape(*dims):
    return jax.ShapeDtypeStruct(dims, jnp.float32)


def swap(block, start):
    count = lax.axis_size("space")
    pairs = [(i, i + 1) for i in range(start, count - 1, 2)]
    return lax.ppermute(block, "space", pairs + [(b, a) for a, b in pairs])


def per_device(tracers, thickness, wind_x, wind_y):
    count, steps = lax.axis_size("tracer"), lax.axis_size("space")
    turn = lambda x: jnp.transpose(x, (0, 2, 1))
    fields = jnp.stack([turn(thickness), turn(wind_x), turn(wind_y)])
    same_chip = [[i, i + 1] for i in range(0, count, 2)]
    pair = lax.all_gather(fields, "tracer", axis_index_groups=same_chip)
    copies = pl.pallas_call(
        spread,
        out_shape=shape(count * SHARE, 128),
        in_specs=[VMEM],
        out_specs=VMEM,
        compiler_params=PARAMS,
    )(pair)
    order = listed(count // 2)
    members = [
        [
            (2 * j + core) * steps + (place + core) % steps
            for j in order
            for core in (LEAD, 1 - LEAD)
        ]
        for place in range(steps)
    ]
    gathered = lax.all_to_all(
        copies.reshape(count, 1, SHARE * 128),
        ("tracer", "space"),
        0,
        0,
        axis_index_groups=members,
    )
    gathered = lax.all_gather(gathered, "tracer", axis_index_groups=same_chip)
    gathered = gathered.reshape(2, count * SHARE, 128)

    flat = tile_rows(tracers)
    once, twice = pl.pallas_call(
        pack_halos,
        out_shape=[shape(LEV, HALO, TR, COLS)] * 2,
        in_specs=[VMEM],
        out_specs=[VMEM] * 2,
        compiler_params=PARAMS,
    )(flat)
    once, twice = swap(once, 0), swap(twice, 1)

    values, thick = pl.pallas_call(
        sweeps,
        out_shape=[shape(TR * LEV * ROWS * 2, 128), shape(LEV, BLOCK, ROWS)],
        in_specs=[VMEM] * 4,
        out_specs=[VMEM] * 2,
        scratch_shapes=[
            pltpu.VMEM((3, 2, LEV * SPAN, 128), jnp.float32),
            pltpu.VMEM((ROWS + HALO, TR, COLS), jnp.float32),
            pltpu.VMEM((4, 7, SPAN, COLS), jnp.float32),
            pltpu.VMEM((LEV * SPAN, COLS), jnp.float32),
            pltpu.VMEM((COLS, LEV * SPAN), jnp.float32),
        ],
        compiler_params=PARAMS,
    )(gathered, flat, twice, once)
    return from_tile_rows(values), turn(thick)


def solution(mesh):
    in_specs = (
        P("tracer", None, "space", None),
        P(None, "space", "tracer"),
        P(None, "space", "tracer"),
        P(None, "space", "tracer"),
    )
    out_specs = (P("tracer", None, "space", None), P(None, "space", "tracer"))
    return jax.shard_map(
        per_device, mesh=mesh, in_specs=in_specs, out_specs=out_specs, check_vma=False
    )
```

```python
import jax
import jax.numpy as jnp
from jax import lax
from jax.experimental import pallas as pl
from jax.experimental.pallas import tpu as pltpu
from jax.sharding import PartitionSpec as P

COURANT_SCALE = 0.025
SUBSTEPS = 2
LEV, ROWS, COLS, TR = 4, 24, 256, 8
LEAD = 1
FIRST = 11
BLOCK = 8
REACH = 3
HALO = 2 * REACH
SIDE = 4
PART = 32
SHARE = 18
SPAN = ROWS + 2 * SIDE
VMEM = pl.BlockSpec(memory_space=pltpu.VMEM)
PARAMS = pltpu.CompilerParams(vmem_limit_bytes=24 * 1024 * 1024)


def listed(chips):
    return [(i + FIRST) % chips for i in range(chips)]


def packed(fields):
    whole = [jnp.concatenate([fields[f, l] for l in range(LEV)], axis=1) for f in range(3)]
    ends = [
        [fields[f, l][:, rows] for f in range(3) for l in range(LEV)]
        for rows in (slice(ROWS - SIDE, ROWS), slice(0, SIDE))
    ]
    thirds = [whole[2][:, n * PART : (n + 1) * PART] for n in range(3)]
    return [
        jnp.concatenate([whole[0], thirds[0]], axis=1),
        jnp.concatenate([whole[1], thirds[1]], axis=1),
        jnp.concatenate([thirds[2]] + ends[0] + ends[1], axis=1),
    ]


def spread(pair, copies):
    core = lax.axis_index("tracer") % 2
    lane = lax.broadcasted_iota(jnp.int32, (BLOCK, 128), 1)
    column = lax.broadcasted_iota(jnp.int32, (BLOCK, 128), 0)
    both = [packed(pair.at[n]) for n in range(2)]
    own = [jnp.where(core == 0, a, b) for a, b in zip(*both)]
    rest = jnp.zeros((BLOCK, 128), jnp.float32)
    for n in range(4):
        moved = pltpu.roll(own[2], n * PART, 1) if n else own[2]
        mine = (lane >= n * PART) & (lane < (n + 1) * PART) & (column % 4 == n)
        rest = jnp.where(mine, moved, rest)
    rest = [jnp.sum(rest[4 * n : 4 * n + 4], axis=0, keepdims=True) for n in range(2)]
    first, second = both[0][2], both[1][2]
    last_rows = jnp.where(lane < 64, pltpu.roll(first, 96, 1), pltpu.roll(second, 32, 1))
    first_rows = jnp.where(lane < 64, pltpu.roll(second, 48, 1), pltpu.roll(first, 112, 1))
    beside = jnp.where(core == 0, last_rows, first_rows)
    half = copies.shape[0] // SHARE // 2
    for i in range(2 * half):
        at = SHARE * i
        same = core == (LEAD if i % 2 == 0 else 1 - LEAD)
        copies[at : at + 8, :] = jnp.where(same, own[0], beside)
        copies[at + 8 : at + 16, :] = own[1]
        copies[at + 16 : at + 17, :] = rest[0]
        copies[at + 17 : at + 18, :] = rest[1]


def tile_rows(x):
    x = x.reshape(TR, LEV, ROWS // 8, 8, COLS // 128, 128)
    return jnp.transpose(x, (0, 1, 2, 4, 3, 5)).reshape(-1, 128)


def from_tile_rows(x):
    x = x.reshape(TR, LEV, ROWS // 8, COLS // 128, 8, 128)
    return jnp.transpose(x, (0, 1, 2, 4, 3, 5)).reshape(TR, LEV, ROWS, COLS)


def row_of_all(l, r, half):
    start = (l * (ROWS // 8) + r // 8) * (COLS // 128) * 8 + half * 8 + r % 8
    return pl.ds(start, TR, stride=LEV * ROWS * (COLS // 128))


def get_row(ref, l, r):
    return jnp.concatenate([ref[row_of_all(l, r, h), :] for h in range(2)], axis=1)


def pack_halos(tracers, once, twice):
    odd = lax.axis_index("space") % 2 == 1
    for l in range(LEV):
        for r in range(HALO):
            low = get_row(tracers, l, r)
            high = get_row(tracers, l, ROWS - HALO + r)
            once[l, r] = jnp.where(odd, low, high)
            twice[l, r] = jnp.where(odd, high, low)


def stencil(courant, flux, after):
    size = jnp.abs(courant)
    rest = 1.0 - size
    part = flux * rest * (1.0 / 12.0)
    near, far = part * rest, part * size
    mean = flux - 12.0 * (near - far)
    up = courant > 0
    far_l = jnp.where(up, far, 0.0)
    far_r = far - far_l
    mean_l = jnp.where(up, mean, 0.0)
    mean_r = mean - mean_l
    near7, left7, right7 = 7.0 * near, 7.0 * far_l, 7.0 * far_r
    outer_l, outer_r = left7 + near, right7 + near
    inner_l = (near7 - left7) + (far_r + mean_l)
    inner_r = (near7 - right7) + (far_l + mean_r)
    return [
        (far_l, 1),
        (outer_l + after(far_l), -1),
        (inner_l + after(outer_l), 1),
        (inner_r - after(inner_l), 1),
        (outer_r + after(inner_r), -1),
        (far_r + after(outer_r), 1),
        (after(far_r), -1),
    ]


def sweeps(
    gathered, tracers, once, twice, out, thick_out, fields, mid, weights, ends, turned
):
    space = lax.axis_index("space")
    tracer = lax.axis_index("tracer")
    last_row = lax.axis_size("space") * ROWS
    odd = space % 2 == 1
    half = gathered.shape[1] // SHARE // 2
    lane = lax.broadcasted_iota(jnp.int32, (BLOCK, 128), 1)
    column = lax.broadcasted_iota(jnp.int32, (BLOCK, 128), 0)
    blocks = [[], [], [], []]
    for chip in range(half):
        j = listed(half).index(chip)
        places = [SHARE * (2 * j + (0 if core == LEAD else 1)) for core in range(2)]
        last_rows = gathered[1, places[0] : places[0] + 8, :]
        first_rows = gathered[0, places[1] : places[1] + 8, :]
        for core, at in enumerate(places):
            blocks[0].append(gathered[core, at : at + 8, :])
            blocks[1].append(gathered[core, at + 8 : at + 16, :])
            rest = [gathered[core, at + 16 + n : at + 17 + n, :] for n in range(2)]
            blocks[2].append(jnp.where(column < 4, rest[0], rest[1]))
        blocks[3].append(jnp.where(lane < 64, last_rows, first_rows))
        blocks[3].append(jnp.where(lane < 64, first_rows, last_rows))
    turned_to = [jnp.concatenate(b, axis=0).T for b in blocks]
    col = lax.broadcasted_iota(jnp.int32, (PART, COLS), 1)
    rest = turned_to[2][:PART]
    for n in range(1, 4):
        rest = jnp.where(col % 4 == n, turned_to[2][n * PART : (n + 1) * PART], rest)
    whole = LEV * ROWS
    own = [turned_to[0][:whole], turned_to[1][:whole]]
    own.append(jnp.concatenate([turned_to[0][whole:], turned_to[1][whole:], rest], axis=0))
    size = 3 * LEV * SIDE
    col = lax.broadcasted_iota(jnp.int32, (size, COLS), 1)
    on_first = (col // BLOCK) % 2 == 0
    low_part, high_part = turned_to[3][:size], turned_to[3][64 : 64 + size]
    below = jnp.where(on_first, low_part, high_part)
    above = jnp.where(on_first, high_part, low_part)
    for f in range(3):
        for l in range(LEV):
            to, side = l * SPAN, (f * LEV + l) * SIDE
            for h in range(2):
                cut = slice(h * 128, (h + 1) * 128)
                fields[f, h, to : to + SIDE, :] = below[side : side + SIDE, cut]
                fields[f, h, to + SIDE : to + SIDE + ROWS, :] = own[f][
                    l * ROWS : (l + 1) * ROWS, cut
                ]
                fields[f, h, to + SIDE + ROWS : to + SPAN, :] = above[
                    side : side + SIDE, cut
                ]

    row = lax.broadcasted_iota(jnp.int32, (SPAN, COLS), 0) + (space * ROWS - SIDE)
    col = lax.broadcasted_iota(jnp.int32, (SPAN, COLS), 1)

    def level(l, carry):
        at = pl.ds(pl.multiple_of(l * SPAN, SPAN), SPAN)
        field = lambda f: jnp.concatenate([fields[f, h, at, :] for h in range(2)], axis=1)
        inside = (row >= 0) & (row < last_row)
        thick = jnp.where(inside, field(0), 1.0)
        next_row = lambda x: pltpu.roll(x, SPAN - 1, 0)
        next_col = lambda x: pltpu.roll(x, COLS - 1, 1)

        cx = jnp.where((row > 0) & (row < last_row), COURANT_SCALE * field(1), 0.0)
        mfx = cx * jnp.where(cx > 0, pltpu.roll(thick, 1, 0), thick)
        cy = jnp.where(inside & (col > 0), COURANT_SCALE * field(2), 0.0)
        mfy = cy * jnp.where(cy > 0, pltpu.roll(thick, 1, 1), thick)
        thin_x = next_row(mfx) - mfx
        thin_y = next_col(mfy) - mfy
        dp1 = thick - thin_x
        dp2 = dp1 - thin_y
        dp3 = dp2 - thin_x
        dp4 = dp3 - thin_y
        ends[at, :] = dp4
        def put(n, adds, starts, results, placed):
            for substep in range(SUBSTEPS):
                over = 1.0 / results[substep]
                signed = {1: over, -1: -over}
                for j, (add, sign) in enumerate(adds):
                    if j == REACH:
                        add = add + starts[substep]
                    weights[2 * substep + n, j] = placed(j - REACH, add * signed[sign])

        def inside_only(adds):
            for j, (add, sign) in enumerate(adds):
                step = j - REACH
                if step < 0:
                    add = jnp.where(col >= -step, add, 0.0)
                elif step > 0:
                    add = jnp.where(col < COLS - step, add, 0.0)
                yield add, sign

        def placed(step, value):
            if abs(step) > 1:
                value = pltpu.roll(value, REACH if step > 0 else COLS - REACH, 1)
            return value

        put(0, stencil(cx, mfx, next_row), (thick, dp2), (dp1, dp3), lambda _, x: x)
        y_adds = list(inside_only(stencil(cy, mfy, next_col)))
        put(1, y_adds, (dp1, dp3), (dp2, dp4), placed)

        def weight(n, j, r):
            return weights[n, j, r + SIDE : r + SIDE + 1, :]

        def along(cells, substep, r):
            total = weight(2 * substep, 0, r) * cells[0]
            for j in range(1, 2 * REACH + 1):
                total += weight(2 * substep, j, r) * cells[j]
            return total

        def begin(q, substep, r):
            w = lambda j: weight(2 * substep + 1, j, r)
            left, right = pltpu.roll(q, 1, 1), next_col(q)
            up = w(0) * q + w(1) * right
            down = w(6) * q + w(5) * left
            return w(3) * q + w(2) * left + w(4) * right, up, down

        def end(total, up, down):
            return total + (pltpu.roll(up, REACH, 1) + pltpu.roll(down, COLS - REACH, 1))

        def first(r):
            if r < 0:
                return jnp.where(odd, once[l, r + HALO], twice[l, r + HALO])
            if r >= ROWS:
                return jnp.where(odd, twice[l, r - ROWS], once[l, r - ROWS])
            return get_row(tracers, l, r)

        def staged(rows, start, stages):
            rows = list(rows)
            held = [dict() for _ in stages]
            for n in range(len(rows) + 14 * (len(stages) - 1)):
                for k, stage in enumerate(stages):
                    at = n - 14 * k
                    if 0 <= at < len(rows):
                        args = held[k - 1].pop(at) if k else start(rows[at])
                        held[k][at] = stage(rows[at], *args)

        def keep_mid(r, *parts):
            mid[r + REACH] = end(*parts)

        def keep_out(r, *parts):
            done = end(*parts)
            for h in range(2):
                out[row_of_all(l, r, h), :] = done[:, h * 128 : (h + 1) * 128]

        window = [first(r) for r in range(-HALO, 0)]

        def next_first(r):
            window.append(first(r + REACH))
            return (list(window[-7:]),)

        staged(
            range(-REACH, ROWS + REACH),
            next_first,
            [
                lambda r, cells: (along(cells, 0, r),),
                lambda r, q: begin(q, 0, r),
                keep_mid,
            ],
        )
        window = [mid[r] for r in range(HALO)]

        def next_mid(r):
            window.append(mid[r + HALO])
            return (list(window[-7:]),)

        staged(
            range(ROWS),
            next_mid,
            [
                lambda r, cells: (along(cells, 1, r),),
                lambda r, q: begin(q, 1, r),
                keep_out,
            ],
        )
        return carry

    lax.fori_loop(0, LEV, level, 0)
    turned[...] = ends[...].T
    block = turned[pl.ds(pl.multiple_of(tracer * BLOCK, BLOCK), BLOCK), :]
    for l in range(LEV):
        start = l * SPAN + SIDE
        thick_out[l] = block[:, start : start + ROWS]


def shape(*dims):
    return jax.ShapeDtypeStruct(dims, jnp.float32)


def swap(block, start):
    count = lax.axis_size("space")
    pairs = [(i, i + 1) for i in range(start, count - 1, 2)]
    return lax.ppermute(block, "space", pairs + [(b, a) for a, b in pairs])


def per_device(tracers, thickness, wind_x, wind_y):
    count, steps = lax.axis_size("tracer"), lax.axis_size("space")
    turn = lambda x: jnp.transpose(x, (0, 2, 1))
    fields = jnp.stack([turn(thickness), turn(wind_x), turn(wind_y)])
    same_chip = [[i, i + 1] for i in range(0, count, 2)]
    pair = lax.all_gather(fields, "tracer", axis_index_groups=same_chip)
    copies = pl.pallas_call(
        spread,
        out_shape=shape(count * SHARE, 128),
        in_specs=[VMEM],
        out_specs=VMEM,
        compiler_params=PARAMS,
    )(pair)
    order = listed(count // 2)
    members = [
        [
            (2 * j + core) * steps + (place + core) % steps
            for j in order
            for core in (LEAD, 1 - LEAD)
        ]
        for place in range(steps)
    ]
    gathered = lax.all_to_all(
        copies.reshape(count, 1, SHARE * 128),
        ("tracer", "space"),
        0,
        0,
        axis_index_groups=members,
    )
    gathered = gathered.reshape(count * SHARE, 128)
    gathered = lax.all_gather(gathered, "tracer", axis_index_groups=same_chip)

    flat = tile_rows(tracers)
    once, twice = pl.pallas_call(
        pack_halos,
        out_shape=[shape(LEV, HALO, TR, COLS)] * 2,
        in_specs=[VMEM],
        out_specs=[VMEM] * 2,
        compiler_params=PARAMS,
    )(flat)
    once, twice = swap(once, 0), swap(twice, 1)

    values, thick = pl.pallas_call(
        sweeps,
        out_shape=[shape(TR * LEV * ROWS * 2, 128), shape(LEV, BLOCK, ROWS)],
        in_specs=[VMEM] * 4,
        out_specs=[VMEM] * 2,
        scratch_shapes=[
            pltpu.VMEM((3, 2, LEV * SPAN, 128), jnp.float32),
            pltpu.VMEM((ROWS + HALO, TR, COLS), jnp.float32),
            pltpu.VMEM((4, 7, SPAN, COLS), jnp.float32),
            pltpu.VMEM((LEV * SPAN, COLS), jnp.float32),
            pltpu.VMEM((COLS, LEV * SPAN), jnp.float32),
        ],
        compiler_params=PARAMS,
    )(gathered, flat, once, twice)
    return from_tile_rows(values), turn(thick)


def solution(mesh):
    in_specs = (
        P("tracer", None, "space", None),
        P(None, "space", "tracer"),
        P(None, "space", "tracer"),
        P(None, "space", "tracer"),
    )
    out_specs = (P("tracer", None, "space", None), P(None, "space", "tracer"))
    return jax.shard_map(
        per_device, mesh=mesh, in_specs=in_specs, out_specs=out_specs, check_vma=False
    )
```
